32 devices in a mesh: member: 4 (over z), lat: 8 (over y, x, core).
Axes of the slice: x: 2, y: 2, z: 4, core: 2. Of those that a mesh axis runs over, the one named last changes fastest.
Arguments:
- grid_input: bfloat16 [4, 384, 768, 256], P('member', 'lat'), may hold values from -6 to 6
- saved_mixed: bfloat16 [4, 384, 768, 256], P('member', 'lat'), may hold values from -6 to 6
- target: bfloat16 [384, 768, 256], P('lat'), may hold values from -6 to 6
- land_weight: int32 [384, 768], P('lat'), may hold values from 0 to 3
- mix_weight: bfloat16 [256, 256], replicated, may hold values from -0.375 to 0.375
- degree_gain: float32 [384], replicated, may hold values from 0.3 to 3
- up_weight: bfloat16 [256, 512], replicated, may hold values from -0.375 to 0.375
- down_weight: bfloat16 [512, 256], replicated, may hold values from -0.25 to 0.25
Outputs:
- grad_input: bfloat16 [4, 384, 768, 256], P('member', 'lat')
The draws below stay inside these ranges and needn't reach their ends.
All inputs are finite; a program needn't handle non-finite values.
Results may differ from the reference program's by a relative error of at most 0.015.
Values may be sent and summed in bfloat16 or wider, within the bound.
No kernel may reach another device: no remote copies, remote signals or barrier semaphores. Data moves between devices by JAX's collectives and lax.ppermute only.
A program may use at most 320 MiB of HBM per device.

```python
import math
import jax
import jax.numpy as jnp
from jax import lax

LATITUDES = 384
LONGITUDES = 768
CHANNELS = 256
HIDDEN_UNITS = 512
WAVENUMBERS = 384
MEMBERS = 4


def touch_ends(result, own_key, low, high):
    longest = result.shape.index(max(result.shape))
    spots = []
    for shift in (0, 1):
        where = [jax.random.randint(jax.random.fold_in(own_key, axis), (), 0, length) for axis, length in enumerate(result.shape)]
        where[longest] = (where[longest] + shift) % result.shape[longest]
        spots.append(tuple(where))
    return result.at[spots[0]].set(low).at[spots[1]].set(high)


def levels(own_key, shape, cuts, smallest, high):
    def one(dim, parts):
        heights = jax.random.uniform(jax.random.fold_in(jax.random.fold_in(own_key, 6), dim), (parts,), jnp.float32, smallest / len(cuts), high / len(cuts))
        return jnp.repeat(jnp.exp(heights), shape[dim] // parts).reshape((-1,) + (1,) * (len(shape) - dim - 1))

    factor_of = one(*cuts[0])
    for cut in cuts[1:]:
        factor_of = factor_of * one(*cut)
    return factor_of


def bell_draw(stream_key, shape, scale, reach, split=(), dtype=jnp.bfloat16):
    entries = jax.random.normal(stream_key, shape, jnp.float32) * scale
    if len(split) > 0:
        entries = levels(stream_key, shape, split, -0.22, 0.18) * entries
    return jnp.clip(entries, min=-reach, max=reach).astype(dtype)


def setup_inputs(seed: int = 0) -> dict:
    arg_keys = jax.random.split(jax.random.key(seed), 9)
    return {
        "grid_input": bell_draw(arg_keys[0], (MEMBERS, LATITUDES, LONGITUDES, CHANNELS), 1.0, 6.0, ((0, 4), (1, 8))),
        "saved_mixed": bell_draw(arg_keys[1], (MEMBERS, LATITUDES, LONGITUDES, CHANNELS), 1.0, 6.0, ((0, 4), (1, 8))),
        "target": bell_draw(arg_keys[2], (LATITUDES, LONGITUDES, CHANNELS), 1.0, 6.0, ((0, 8),)),
        "land_weight": touch_ends(jax.random.randint(arg_keys[3], (LATITUDES, LONGITUDES), 0, 4), jax.random.fold_in(arg_keys[3], 1), 0, 3).astype(jnp.int32),
        "mix_weight": bell_draw(arg_keys[4], (CHANNELS, CHANNELS), CHANNELS ** -0.5, 0.375),
        "degree_gain": jnp.clip(jnp.exp(jax.random.uniform(arg_keys[5], (LATITUDES,), jnp.float32, math.log(0.3), math.log(3.0))), 0.3, 3.0),
        "up_weight": bell_draw(arg_keys[6], (CHANNELS, HIDDEN_UNITS), CHANNELS ** -0.5, 0.375),
        "down_weight": bell_draw(arg_keys[7], (HIDDEN_UNITS, CHANNELS), HIDDEN_UNITS ** -0.5, 0.25),
    }


kappa_gelu = 0.7978845608
cubic_gelu = 0.044715
smooth_square = 0.25

def gelu_parts(inputs):
    tanh_part = jnp.tanh(kappa_gelu * (inputs + cubic_gelu * inputs * inputs * inputs))
    values = 0.5 * inputs * (1.0 + tanh_part)
    slopes = 0.5 * (1.0 + tanh_part) + 0.5 * inputs * (1.0 - tanh_part * tanh_part) * kappa_gelu * (1.0 + 3.0 * cubic_gelu * inputs * inputs)
    return (values, slopes)

def slope_abs(difference):
    return difference * lax.rsqrt(difference * difference + smooth_square)

def member_term(own_values, everyone, target, weights):
    member_count = everyone.shape[0]
    total = jnp.zeros(own_values.shape, jnp.float32)
    for slot in range(member_count):
        total = total + slope_abs(own_values - everyone[slot].astype(jnp.float32))
    direct = slope_abs(own_values - target.astype(jnp.float32))
    return (weights * (direct / member_count - total / (member_count * member_count))).astype(jnp.bfloat16)

def fourier_tables(lon_count, mode_count):
    positions = jnp.arange(lon_count)
    orders = jnp.arange(mode_count)
    phase = positions[:, None] * orders[None, :] % lon_count
    angle_grid = phase.astype(jnp.float32) * (2.0 * math.pi / lon_count)
    cosine = jnp.cos(angle_grid)
    sine = jnp.sin(angle_grid)
    factor = jnp.where(orders == 0, 1.0, 2.0).astype(jnp.float32)
    synth_table = jnp.concatenate([cosine * factor[None, :], -sine * factor[None, :]], axis=1).astype(jnp.bfloat16)
    analysis_table = jnp.concatenate([cosine.T, -sine.T], axis=0).astype(jnp.bfloat16)
    return (synth_table, analysis_table)

def legendre_table(orders, lat_count, degree_count):
    angles = (jnp.arange(lat_count).astype(jnp.float32) + 0.5) * (math.pi / lat_count)
    cosine = jnp.cos(angles)
    sine = jnp.sin(angles)
    order_f = orders.astype(jnp.float32)[:, None]
    factor_index = jnp.arange(1, lat_count + 1).astype(jnp.float32)
    ratios = jnp.log((2.0 * factor_index - 1.0) / (2.0 * factor_index))
    partial_log = lax.optimization_barrier(jnp.sum(jnp.where(factor_index[None, :] <= order_f, ratios[None, :], 0.0), axis=1))
    start_log = 0.5 * jnp.log(order_f + 0.5) + 0.5 * partial_log[:, None] + order_f * jnp.log(sine)[None, :]
    zeros_start = jnp.zeros((orders.shape[0], lat_count), jnp.float32)

    def advance(state, degree):
        older, newer, log_scale = state
        degree_f = degree.astype(jnp.float32)
        alpha_rec = jnp.sqrt(jnp.maximum(4.0 * degree_f * degree_f - 1.0, 1.0) / jnp.maximum(degree_f * degree_f - order_f * order_f, 1.0))
        below = degree_f - 1.0
        beta_rec = jnp.sqrt(jnp.maximum(below * below - order_f * order_f, 0.0) / jnp.maximum(4.0 * below * below - 1.0, 1.0))
        recurred = alpha_rec * (cosine[None, :] * newer - beta_rec * older)
        fresh = jnp.where(degree_f < order_f, 0.0, jnp.where(degree_f == order_f, 1.0, recurred))
        output = fresh * jnp.exp(log_scale)
        norm_value = jnp.where(degree_f < order_f, 1.0, jnp.maximum(jnp.abs(fresh), jnp.abs(newer)))
        return ((newer / norm_value, fresh / norm_value, log_scale + jnp.log(norm_value)), output)
    block_size = math.gcd(degree_count, 32)

    def advance_block(state, block_start):
        rows_out = []
        for offset in range(block_size):
            state, output = advance(state, block_start + offset)
            rows_out.append(output)
        return (state, jnp.stack(rows_out))
    start_state = (zeros_start, zeros_start, start_log + zeros_start)
    block_starts = (jnp.arange(degree_count // block_size) * block_size).astype(jnp.int32)
    final_state, table_blocks = lax.scan(advance_block, start_state, block_starts)
    return table_blocks.reshape(degree_count, orders.shape[0], lat_count)

def widen(array_low):
    return lax.optimization_barrier(array_low).astype(jnp.float32)

def mlp_branch(saved_one, up_weight, down_weight):
    flat_saved = saved_one.reshape(-1, saved_one.shape[-1])
    hidden_pre = jnp.dot(flat_saved, up_weight, preferred_element_type=jnp.float32)
    values, slopes = gelu_parts(hidden_pre)
    activation = values.astype(jnp.bfloat16)
    return (jnp.dot(activation, down_weight, preferred_element_type=jnp.float32), slopes)

def reference(grid_input, saved_mixed, target, land_weight, mix_weight, degree_gain, up_weight, down_weight):
    synth_table, analysis_table = fourier_tables(LONGITUDES, WAVENUMBERS)
    legendre = widen(legendre_table(jnp.arange(WAVENUMBERS), LATITUDES, LATITUDES).astype(jnp.bfloat16))
    angles = (jnp.arange(LATITUDES).astype(jnp.float32) + 0.5) * (math.pi / LATITUDES)
    quad_weight = jnp.sin(angles) * (math.pi / LATITUDES)
    weights = (jnp.sin(angles)[:, None] * land_weight.astype(jnp.float32))[:, :, None]

    def forward_member(pair):
        grid_one, saved_one = pair
        branch_out, unused_slopes = mlp_branch(saved_one, up_weight, down_weight)
        summed = grid_one.reshape(branch_out.shape).astype(jnp.float32) + branch_out
        return summed.astype(jnp.bfloat16).reshape(grid_one.shape)
    everyone = lax.map(forward_member, (grid_input, saved_mixed))
    cotangents = jnp.stack([member_term(everyone[slot].astype(jnp.float32), everyone, target, weights) for slot in range(MEMBERS)])

    def backward_member(pair):
        saved_one, cotangent = pair
        unused_branch, slopes = mlp_branch(saved_one, up_weight, down_weight)
        act_grad = jnp.dot(cotangent.reshape(-1, CHANNELS), down_weight.T, preferred_element_type=jnp.float32)
        pre_grad = (act_grad * slopes).astype(jnp.bfloat16)
        mixed_grad = jnp.dot(pre_grad, up_weight.T, preferred_element_type=jnp.float32).astype(jnp.bfloat16)
        mixed_grad = mixed_grad.reshape(LATITUDES, LONGITUDES, CHANNELS)
        wave_grad = jnp.einsum('jnc,nk->jkc', widen(mixed_grad), synth_table.astype(jnp.float32)).astype(jnp.bfloat16)
        wave_grad = wave_grad.reshape(LATITUDES, 2, WAVENUMBERS, CHANNELS)
        degree_grad = jnp.einsum('lmj,jpmc->lpmc', legendre, widen(wave_grad))
        gained = (degree_grad * degree_gain[:, None, None, None]).astype(jnp.bfloat16)
        coeff_grad = jnp.einsum('lpmd,cd->lpmc', widen(gained), mix_weight.astype(jnp.float32)).astype(jnp.bfloat16)
        lat_grad = jnp.einsum('lmj,lpmc->jpmc', legendre, widen(coeff_grad)) * quad_weight[:, None, None, None]
        lat_grad = lat_grad.astype(jnp.bfloat16).reshape(LATITUDES, 2 * WAVENUMBERS, CHANNELS)
        spatial = jnp.einsum('jkc,kn->jnc', widen(lat_grad), analysis_table.astype(jnp.float32)) * (1.0 / LONGITUDES)
        return (cotangent.astype(jnp.float32) + spatial).astype(jnp.bfloat16)
    return lax.map(backward_member, (saved_mixed, cotangents))
```

```python
import functools
import math

import jax
import jax.numpy as jnp
from jax import lax
from jax.experimental import pallas as pl
from jax.experimental.pallas import tpu as pltpu
from jax.sharding import PartitionSpec as P

kappa_gelu = 0.7978845608
cubic_gelu = 0.044715
smooth_square = 0.25
F32 = jnp.float32
BF16 = jnp.bfloat16
PARAMS = pltpu.CompilerParams(vmem_limit_bytes=48 * 1024 * 1024)


TOKEN = jax.ShapeDtypeStruct((8, 128), F32)
TOKEN_IN = pl.BlockSpec(memory_space=pl.ANY)
TOKEN_OUT = pl.BlockSpec((8, 128), lambda *_: (0, 0))


def put_token(token_ref):
    token_ref[...] = jnp.zeros_like(token_ref)


def dot(a, b):
    return jnp.dot(a, b, preferred_element_type=F32)


def slope_abs(difference):
    return difference * lax.rsqrt(difference * difference + smooth_square)


def fourier_tables(lon_count, mode_count):
    row = jnp.arange(2 * mode_count)
    part = row // mode_count
    orders = row % mode_count
    positions = jnp.arange(lon_count)
    phase = orders[:, None] * positions[None, :] % lon_count
    angle_grid = phase.astype(F32) * (2.0 * math.pi / lon_count)
    values = jnp.where(part[:, None] == 0, jnp.cos(angle_grid), -jnp.sin(angle_grid))
    factor = jnp.where(orders == 0, 1.0, 2.0).astype(F32)
    synth = (values * factor[:, None]).astype(BF16)
    return synth, values.T.astype(BF16)


def legendre_kernel(
    start_ref, cosine_ref, order_ref, _, out_ref, token_ref, older_ref, newer_ref, log_ref, rows_ref
):
    put_token(token_ref)
    block = out_ref.shape[1]
    order = order_ref[...]
    cosine = cosine_ref[...]

    @pl.when(pl.program_id(0) == 0)
    def _():
        older_ref[...] = jnp.zeros_like(older_ref)
        newer_ref[...] = jnp.zeros_like(newer_ref)
        log_ref[...] = start_ref[...]

    for offset in range(block):
        degree = (pl.program_id(0) * block + offset).astype(F32)
        below = degree - 1.0
        alpha = jnp.sqrt(
            jnp.maximum(4.0 * degree * degree - 1.0, 1.0)
            / jnp.maximum(degree * degree - order * order, 1.0)
        )
        beta = jnp.sqrt(
            jnp.maximum(below * below - order * order, 0.0)
            / jnp.maximum(4.0 * below * below - 1.0, 1.0)
        )
        newer = newer_ref[...]
        log_scale = log_ref[...]
        recurred = alpha * (cosine * newer - beta * older_ref[...])
        fresh = jnp.where(degree < order, 0.0, jnp.where(degree == order, 1.0, recurred))
        rows_ref[:, offset, :] = fresh * jnp.exp(log_scale)
        norm = jnp.where(degree < order, 1.0, jnp.maximum(jnp.abs(fresh), jnp.abs(newer)))
        older_ref[...] = newer / norm
        newer_ref[...] = fresh / norm
        log_ref[...] = log_scale + jnp.log(norm)
    out_ref[...] = rows_ref[...].astype(BF16)


def legendre_table(token, orders, angles, degree_count):
    lat_count = angles.shape[0]
    order_count = orders.shape[0]
    order_f = orders.astype(F32)[:, None]
    factor_index = jnp.arange(1, lat_count + 1).astype(F32)
    ratios = jnp.log((2.0 * factor_index - 1.0) / (2.0 * factor_index))
    partial_log = jnp.sum(jnp.where(factor_index[None, :] <= order_f, ratios[None, :], 0.0), axis=1)
    start_log = (
        0.5 * jnp.log(order_f + 0.5)
        + 0.5 * partial_log[:, None]
        + order_f * jnp.log(jnp.sin(angles))[None, :]
    )
    block = math.gcd(degree_count, 16)
    state = pltpu.VMEM((order_count, lat_count), F32)
    return pl.pallas_call(
        legendre_kernel,
        grid=(degree_count // block,),
        in_specs=[
            pl.BlockSpec((order_count, lat_count), lambda i: (0, 0)),
            pl.BlockSpec((1, lat_count), lambda i: (0, 0)),
            pl.BlockSpec((order_count, 1), lambda i: (0, 0)),
            TOKEN_IN,
        ],
        out_specs=[
            pl.BlockSpec((order_count, block, lat_count), lambda i: (0, i, 0)),
            TOKEN_OUT,
        ],
        out_shape=[
            jax.ShapeDtypeStruct((order_count, degree_count, lat_count), BF16),
            TOKEN,
        ],
        scratch_shapes=[state, state, state, pltpu.VMEM((order_count, block, lat_count), F32)],
        compiler_params=PARAMS,
        cost_estimate=pl.CostEstimate(
            flops=40 * order_count * degree_count * lat_count,
            bytes_accessed=2 * order_count * degree_count * lat_count,
            transcendentals=4 * order_count * degree_count * lat_count,
        ),
    )(start_log, jnp.cos(angles)[None, :], order_f, token)


def share_of(me_ref, piece, members, share):
    return pl.ds(pl.multiple_of(lax.rem(me_ref[0] + piece, members) * share, share), share)


def forward_kernel(me_ref, saved_ref, grid_ref, up_ref, down_ref, _, *out_refs):
    put_token(out_refs[-1])
    out_refs = out_refs[:-1]
    members = len(out_refs)
    share = out_refs[0].shape[1]
    for piece in range(members):
        place = share_of(me_ref, piece, members, share)
        v = dot(saved_ref[0, place, :], up_ref[...])
        tanh_part = jnp.tanh(kappa_gelu * (v + cubic_gelu * v * v * v))
        activation = (0.5 * v * (1.0 + tanh_part)).astype(BF16)
        total = grid_ref[0, place, :].astype(F32) + dot(activation, down_ref[...])
        out_refs[piece][0] = total.astype(BF16)


def forward_rows(token, first, rows, members, me, saved, grid_input, up_weight, down_weight):
    _, lon, channels = saved.shape
    hidden = up_weight.shape[1]
    share = lon // members
    row_spec = pl.BlockSpec((1, lon, channels), lambda i, q: (first + i, 0, 0))
    piece_spec = pl.BlockSpec((1, share, channels), lambda i, q: (i, 0, 0))
    return pl.pallas_call(
        forward_kernel,
        grid_spec=pltpu.PrefetchScalarGridSpec(
            num_scalar_prefetch=1,
            grid=(rows,),
            in_specs=[
                row_spec,
                row_spec,
                pl.BlockSpec((channels, hidden), lambda i, q: (0, 0)),
                pl.BlockSpec((hidden, channels), lambda i, q: (0, 0)),
                TOKEN_IN,
            ],
            out_specs=[piece_spec] * members + [TOKEN_OUT],
        ),
        out_shape=[jax.ShapeDtypeStruct((rows, share, channels), BF16)] * members + [TOKEN],
        compiler_params=PARAMS,
        cost_estimate=pl.CostEstimate(
            flops=4 * rows * lon * channels * hidden,
            bytes_accessed=6 * rows * lon * channels,
            transcendentals=rows * lon * hidden,
        ),
    )(me, saved, grid_input, up_weight, down_weight, token)


def cotangent_kernel(first, members, me_ref, target_ref, weight_ref, _, *refs):
    put_token(refs[-1])
    row = first + pl.program_id(0)
    weight_block = weight_ref[...]
    lane = lax.broadcasted_iota(jnp.int32, weight_block.shape, 1)
    weight = jnp.sum(jnp.where(lane == row, weight_block, 0.0), axis=1, keepdims=True)
    target = target_ref[0].astype(F32)
    values = [refs[e][0].astype(F32) for e in range(members)]
    pairs = {}
    for e in range(members):
        for f in range(e + 1, members):
            pairs[e, f] = slope_abs(values[e] - values[f])
    for e in range(members):
        total = None
        for f in range(members):
            if f == e:
                continue
            term = pairs[e, f] if e < f else -pairs[f, e]
            total = term if total is None else total + term
        direct = slope_abs(values[e] - target)
        refs[members + e][0] = (
            weight * (direct * (1.0 / members) - total * (1.0 / (members * members)))
        ).astype(BF16)


def cotangent_rows(token, first, me, pieces, target, weights):
    members = len(pieces)
    rows, share, channels = pieces[0].shape
    piece_spec = pl.BlockSpec((1, share, channels), lambda i, q: (i, 0, 0))
    return pl.pallas_call(
        functools.partial(cotangent_kernel, first, members),
        grid_spec=pltpu.PrefetchScalarGridSpec(
            num_scalar_prefetch=1,
            grid=(rows,),
            in_specs=[
                pl.BlockSpec((1, share, channels), lambda i, q: (first + i, q[0], 0)),
                pl.BlockSpec((share, weights.shape[1]), lambda i, q: (q[0], 0)),
                TOKEN_IN,
            ]
            + [piece_spec] * members,
            out_specs=[piece_spec] * members + [TOKEN_OUT],
        ),
        out_shape=[jax.ShapeDtypeStruct(pieces[0].shape, BF16)] * members + [TOKEN],
        compiler_params=PARAMS,
        cost_estimate=pl.CostEstimate(
            flops=80 * rows * share * channels,
            bytes_accessed=(4 * members + 2) * rows * share * channels,
            transcendentals=10 * rows * share * channels,
        ),
    )(me, target, weights, token, *pieces)


def backward_kernel(me_ref, saved_ref, up_ref, down_t_ref, up_t_ref, synth_ref, _, __, *refs):
    members = len(refs) - 4
    out_ref, token_ref, mixed_ref, waves_ref = refs[members:]
    put_token(token_ref)
    lon, channels = mixed_ref.shape
    share = lon // members
    for piece in range(members):
        place = share_of(me_ref, piece, members, share)
        v = dot(saved_ref[0, place, :], up_ref[...])
        square = v * v
        t = jnp.tanh(kappa_gelu * (v + cubic_gelu * square * v))
        slopes = 0.5 * (1.0 + t) + 0.5 * v * (1.0 - t * t) * kappa_gelu * (
            1.0 + 3.0 * cubic_gelu * square
        )
        act_grad = dot(refs[piece][0], down_t_ref[...])
        pre_grad = (act_grad * slopes).astype(BF16)
        mixed_ref[place, :] = dot(pre_grad, up_t_ref[...]).astype(BF16)
    wave = dot(synth_ref[...], mixed_ref[...])
    modes = wave.shape[0] // 2
    row = pl.program_id(0)
    waves_ref[:, row, :channels] = wave[:modes]
    waves_ref[:, row, channels:] = wave[modes:]

    @pl.when(row == pl.num_programs(0) - 1)
    def _():
        out_ref[...] = waves_ref[...].astype(BF16).reshape(out_ref.shape)


def backward_rows(token, ahead, first, groups, me, cot, saved, up_weight, down_t, up_t, synth):
    members = len(cot)
    rows, share, channels = cot[0].shape
    lon = saved.shape[1]
    hidden = up_weight.shape[1]
    modes = synth.shape[0] // 2
    whole = lambda a: pl.BlockSpec(a.shape, lambda i, q: (0, 0))
    piece_spec = pl.BlockSpec((1, share, channels), lambda i, q: (i, 0, 0))
    out_shape = (groups, modes // groups, rows, 2 * channels)
    return pl.pallas_call(
        backward_kernel,
        grid_spec=pltpu.PrefetchScalarGridSpec(
            num_scalar_prefetch=1,
            grid=(rows,),
            in_specs=[
                pl.BlockSpec((1, lon, channels), lambda i, q: (first + i, 0, 0)),
                whole(up_weight),
                whole(down_t),
                whole(up_t),
                whole(synth),
                TOKEN_IN,
                TOKEN_IN,
            ]
            + [piece_spec] * members,
            out_specs=[pl.BlockSpec(out_shape, lambda i, q: (0, 0, 0, 0)), TOKEN_OUT],
            scratch_shapes=[
                pltpu.VMEM((lon, channels), BF16),
                pltpu.VMEM((modes, rows, 2 * channels), F32),
            ],
        ),
        out_shape=[jax.ShapeDtypeStruct(out_shape, BF16), TOKEN],
        compiler_params=PARAMS,
        cost_estimate=pl.CostEstimate(
            flops=rows * lon * channels * (6 * hidden + 4 * modes),
            bytes_accessed=6 * rows * lon * channels,
            transcendentals=rows * lon * hidden,
        ),
    )(me, saved, up_weight, down_t, up_t, synth, token, ahead, *cot)


def spectral_kernel(parts, table_ref, gain_ref, mix_t_ref, _, *refs):
    out_ref, token_ref = refs[parts:]
    put_token(token_ref)
    channels = mix_t_ref.shape[0]
    batch, columns = refs[0].shape[1], refs[0].shape[-1]
    for m in range(batch):
        pieces = [refs[p][:, m].astype(F32).reshape(-1, columns) for p in range(parts)]
        wave = jnp.concatenate(pieces, axis=0).astype(BF16)
        gained = (dot(table_ref[m], wave) * gain_ref[...]).astype(BF16)
        out_ref[m, :, :channels] = dot(gained[:, :channels], mix_t_ref[...]).astype(BF16)
        out_ref[m, :, channels:] = dot(gained[:, channels:], mix_t_ref[...]).astype(BF16)


def spectral(token, table, gain, mix_t, waves):
    parts = len(waves)
    groups, modes, rows, columns = waves[0].shape
    degrees, lats = table.shape[1:]
    batch = math.gcd(modes, 4)
    return pl.pallas_call(
        functools.partial(spectral_kernel, parts),
        grid=(modes // batch,),
        in_specs=[
            pl.BlockSpec((batch, degrees, lats), lambda m: (m, 0, 0)),
            pl.BlockSpec(gain.shape, lambda m: (0, 0)),
            pl.BlockSpec(mix_t.shape, lambda m: (0, 0)),
            TOKEN_IN,
        ]
        + [pl.BlockSpec((groups, batch, rows, columns), lambda m: (0, m, 0, 0))] * parts,
        out_specs=[pl.BlockSpec((batch, degrees, columns), lambda m: (m, 0, 0)), TOKEN_OUT],
        out_shape=[jax.ShapeDtypeStruct((modes, degrees, columns), BF16), TOKEN],
        compiler_params=PARAMS,
        cost_estimate=pl.CostEstimate(
            flops=modes * columns * degrees * (2 * lats + columns),
            bytes_accessed=modes * (2 * lats * degrees + 2 * columns * (lats + degrees)),
            transcendentals=0,
        ),
    )(table, gain, mix_t, token, *waves)


def latitude_kernel(joined, table_ref, quad_ref, coeff_ref, _, out_ref, token_ref):
    put_token(token_ref)
    groups, batch, rows, columns = out_ref.shape
    for m in range(batch):
        lat = lax.dot_general(
            table_ref[m], coeff_ref[m], (((0,), (0,)), ((), ())), preferred_element_type=F32
        )
        lat = (lat * quad_ref[...]).reshape(joined, groups, rows // joined, columns)
        out_ref[:, m] = jnp.concatenate([lat[p] for p in range(joined)], axis=1).astype(BF16)


def latitude_rows(token, index, joined, groups, table, quad, coeff):
    modes, degrees, columns = coeff.shape
    lats = quad.shape[0]
    batch = math.gcd(modes, 4)
    out_shape = (groups, modes, lats // groups, columns)
    return pl.pallas_call(
        functools.partial(latitude_kernel, joined),
        grid=(modes // batch,),
        in_specs=[
            pl.BlockSpec((batch, degrees, lats), lambda m: (m, 0, index)),
            pl.BlockSpec(quad.shape, lambda m: (0, 0)),
            pl.BlockSpec((batch, degrees, columns), lambda m: (m, 0, 0)),
            TOKEN_IN,
        ],
        out_specs=[
            pl.BlockSpec((groups, batch, lats // groups, columns), lambda m: (0, m, 0, 0)),
            TOKEN_OUT,
        ],
        out_shape=[jax.ShapeDtypeStruct(out_shape, BF16), TOKEN],
        compiler_params=PARAMS,
        cost_estimate=pl.CostEstimate(
            flops=2 * modes * columns * degrees * lats,
            bytes_accessed=2 * modes * (lats * degrees + columns * (lats + degrees)),
            transcendentals=0,
        ),
    )(table, quad, coeff, token)


def output_kernel(joined, members, scale, me_ref, wave_ref, analysis_ref, _, *refs):
    out_ref, token_ref, waves_ref = refs[-3:]
    put_token(token_ref)
    rows, share = wave_ref.shape[2] // joined, refs[0].shape[1]
    channels = out_ref.shape[-1]
    row = pl.program_id(0)

    @pl.when(row == 0)
    def _():
        waves_ref[...] = wave_ref[...].astype(F32).reshape(waves_ref.shape)

    wave = jnp.concatenate(
        [waves_ref[:, row, :channels].astype(BF16), waves_ref[:, row, channels:].astype(BF16)],
        axis=0,
    )
    for piece in range(members):
        place = share_of(me_ref, piece, members, share)
        spatial = dot(analysis_ref[place, :], wave)
        cot = refs[piece][0]
        for part in range(1, joined):
            cot = jnp.where(row >= part * rows, refs[part * members + piece][0], cot)
        out_ref[0, 0, place, :] = (cot.astype(F32) + spatial * scale).astype(BF16)


def output_rows(token, index, shape, me, wave, cots, analysis, held):
    groups, modes, rows, columns = wave.shape
    joined, members = len(cots), len(cots[0])
    each, share, channels = cots[0][0].shape
    lon = shape[2]
    in_specs = [
        pl.BlockSpec(wave.shape, lambda i, q: (0, 0, 0, 0)),
        pl.BlockSpec(analysis.shape, lambda i, q: (0, 0)),
        TOKEN_IN,
    ]
    operands = [me, wave, analysis, token]
    for part, cot in enumerate(cots):
        place = lambda i, q, part=part: (jnp.clip(i - part * each, 0, each - 1), 0, 0)
        in_specs += [pl.BlockSpec((1, share, channels), place)] * members
        operands += cot
    aliases = {}
    if held is not None:
        in_specs.append(pl.BlockSpec(memory_space=pl.ANY))
        aliases = {len(operands): 0}
        operands.append(held)
    return pl.pallas_call(
        functools.partial(output_kernel, joined, members, 1.0 / lon),
        grid_spec=pltpu.PrefetchScalarGridSpec(
            num_scalar_prefetch=1,
            grid=(rows,),
            in_specs=in_specs,
            out_specs=[
                pl.BlockSpec((1, 1, lon, channels), lambda i, q: (0, index * rows + i, 0, 0)),
                TOKEN_OUT,
            ],
            scratch_shapes=[pltpu.VMEM((groups * modes, rows, columns), F32)],
        ),
        out_shape=[jax.ShapeDtypeStruct(shape, BF16), TOKEN],
        input_output_aliases=aliases,
        compiler_params=PARAMS,
        cost_estimate=pl.CostEstimate(
            flops=2 * rows * lon * groups * modes * columns,
            bytes_accessed=6 * rows * lon * channels,
            transcendentals=0,
        ),
    )(*operands)


def shift(pieces, step):
    members = len(pieces)
    moved = [pieces[0]]
    for piece in range(1, members):
        pairs = [(e, (e + step * piece) % members) for e in range(members)]
        moved.append(lax.ppermute(pieces[piece], "member", pairs))
    return moved


def kernel_order(parts):
    order = [("forward", 0), ("forward", 1), ("table", 0), ("forward", 2)]
    for part in range(parts + 1):
        order += [("cotangent", part), ("backward", part - 1), ("forward", part + 3)]
    return [(kind, part) for kind, part in order if 0 <= part < parts]


def shards(
    grid_input, saved_mixed, target, land_weight, mix_weight, degree_gain, up_weight, down_weight
):
    rows_lat, lon_count, channel_count = grid_input.shape[1:]
    total_lat = degree_gain.shape[0]
    mode_count = lon_count // 2
    members = lax.axis_size("member")
    groups = lax.axis_size("lat")
    local_modes = mode_count // groups
    parts = math.gcd(rows_lat, 6)
    rows = rows_lat // parts
    starts = [part * rows for part in range(parts)]

    grid_rows = grid_input[0]
    saved_rows = saved_mixed[0]
    down_t = down_weight.T
    up_t = up_weight.T
    synth, analysis = fourier_tables(lon_count, mode_count)
    lat_start = lax.axis_index("lat") * rows_lat
    local_angles = ((lat_start + jnp.arange(rows_lat)).astype(F32) + 0.5) * (math.pi / total_lat)
    weights = (jnp.sin(local_angles)[:, None] * land_weight.astype(F32)).T
    me = lax.axis_index("member").astype(jnp.int32).reshape(1)

    lats = jnp.arange(total_lat).reshape(groups, parts, rows).swapaxes(0, 1).reshape(-1)
    angles = (lats.astype(F32) + 0.5) * (math.pi / total_lat)
    quad_weight = (jnp.sin(angles) * (math.pi / total_lat))[:, None]
    local_orders = lax.axis_index("lat") * local_modes + jnp.arange(local_modes)

    joined = 2 if parts % 2 == 0 else 1
    token = jnp.zeros(TOKEN.shape, F32)
    values, cots, waves = {}, {}, {}
    table = None
    for kind, part in kernel_order(parts):
        if kind == "table":
            table, token = legendre_table(token, local_orders, angles, total_lat)
        elif kind == "forward":
            *pieces, token = forward_rows(
                token, starts[part], rows, members, me, saved_rows, grid_rows, up_weight, down_weight
            )
            values[part] = shift(pieces, 1)
        elif kind == "cotangent":
            *pieces, token = cotangent_rows(token, starts[part], me, values[part], target, weights)
            cots[part] = shift(pieces, -1)
        else:
            wave, token = backward_rows(
                token,
                waves.get(part - 1, token),
                starts[part],
                groups,
                me,
                cots[part],
                saved_rows,
                up_weight,
                down_t,
                up_t,
                synth,
            )
            waves[part] = lax.all_to_all(wave, "lat", 0, 0, tiled=True)
    waves = [waves[part] for part in range(parts)]
    coeff, token = spectral(token, table, degree_gain[:, None], mix_weight.T, waves)
    result = None
    steps = parts // joined
    lat_waves = {}
    for step in range(steps + 1):
        if step < steps:
            quad = lax.slice_in_dim(quad_weight, step * total_lat // steps, (step + 1) * total_lat // steps)
            wave, token = latitude_rows(token, step, joined, groups, table, quad, coeff)
            lat_waves[step] = lax.all_to_all(wave, "lat", 0, 0, tiled=True)
        if step > 0:
            result, token = output_rows(
                token,
                step - 1,
                grid_input.shape,
                me,
                lat_waves[step - 1],
                [cots[part] for part in range((step - 1) * joined, step * joined)],
                analysis,
                result,
            )
    return result


def solution(mesh):
    in_specs = (
        P("member", "lat", None, None),
        P("member", "lat", None, None),
        P("lat", None, None),
        P("lat", None),
        P(),
        P(),
        P(),
        P(),
    )
    out_specs = P("member", "lat", None, None)
    return jax.shard_map(shards, mesh=mesh, in_specs=in_specs, out_specs=out_specs, check_vma=False)
```

```python
import functools
import math

import jax
import jax.numpy as jnp
from jax import lax
from jax.experimental import pallas as pl
from jax.experimental.pallas import tpu as pltpu
from jax.sharding import PartitionSpec as P

kappa_gelu = 0.7978845608
cubic_gelu = 0.044715
smooth_square = 0.25
F32 = jnp.float32
BF16 = jnp.bfloat16
PARAMS = pltpu.CompilerParams(vmem_limit_bytes=48 * 1024 * 1024)


TOKEN = jax.ShapeDtypeStruct((8, 128), F32)
TOKEN_IN = pl.BlockSpec(memory_space=pl.ANY)
TOKEN_OUT = pl.BlockSpec((8, 128), lambda *_: (0, 0))


def strips(rows, columns):
    lanes = math.gcd(columns // 2, 128)
    return pltpu.VMEM((columns // lanes, rows, lanes), F32)


def put_token(token_ref):
    token_ref[...] = jnp.zeros_like(token_ref)


COST = pl.CostEstimate(flops=5 * 10**10, bytes_accessed=1000, transcendentals=0)


def dot(a, b):
    return jnp.dot(a, b, preferred_element_type=F32)


def slope_abs(difference):
    return difference * lax.rsqrt(difference * difference + smooth_square)


def fourier_tables(lon_count, mode_count):
    row = jnp.arange(2 * mode_count)
    part = row // mode_count
    orders = row % mode_count
    positions = jnp.arange(lon_count)
    phase = orders[:, None] * positions[None, :] % lon_count
    angle_grid = phase.astype(F32) * (2.0 * math.pi / lon_count)
    values = jnp.where(part[:, None] == 0, jnp.cos(angle_grid), -jnp.sin(angle_grid))
    factor = jnp.where(orders == 0, 1.0, 2.0).astype(F32)
    synth = (values * factor[:, None]).astype(BF16)
    return synth, values.T.astype(BF16)


def legendre_kernel(
    start_ref, cosine_ref, order_ref, _, out_ref, token_ref, older_ref, newer_ref, log_ref, rows_ref
):
    put_token(token_ref)
    block = out_ref.shape[1]
    order = order_ref[...]
    cosine = cosine_ref[...]

    @pl.when(pl.program_id(0) == 0)
    def _():
        older_ref[...] = jnp.zeros_like(older_ref)
        newer_ref[...] = jnp.zeros_like(newer_ref)
        log_ref[...] = start_ref[...]

    for offset in range(block):
        degree = (pl.program_id(0) * block + offset).astype(F32)
        below = degree - 1.0
        alpha = jnp.sqrt(
            jnp.maximum(4.0 * degree * degree - 1.0, 1.0)
            / jnp.maximum(degree * degree - order * order, 1.0)
        )
        beta = jnp.sqrt(
            jnp.maximum(below * below - order * order, 0.0)
            / jnp.maximum(4.0 * below * below - 1.0, 1.0)
        )
        newer = newer_ref[...]
        log_scale = log_ref[...]
        recurred = alpha * (cosine * newer - beta * older_ref[...])
        fresh = jnp.where(degree < order, 0.0, jnp.where(degree == order, 1.0, recurred))
        rows_ref[:, offset, :] = fresh * jnp.exp(log_scale)
        norm = jnp.where(degree < order, 1.0, jnp.maximum(jnp.abs(fresh), jnp.abs(newer)))
        older_ref[...] = newer / norm
        newer_ref[...] = fresh / norm
        log_ref[...] = log_scale + jnp.log(norm)
    out_ref[...] = rows_ref[...].astype(BF16)


def legendre_table(token, orders, angles, degree_count):
    lat_count = angles.shape[0]
    order_count = orders.shape[0]
    order_f = orders.astype(F32)[:, None]
    factor_index = jnp.arange(1, lat_count + 1).astype(F32)
    ratios = jnp.log((2.0 * factor_index - 1.0) / (2.0 * factor_index))
    partial_log = jnp.sum(jnp.where(factor_index[None, :] <= order_f, ratios[None, :], 0.0), axis=1)
    start_log = (
        0.5 * jnp.log(order_f + 0.5)
        + 0.5 * partial_log[:, None]
        + order_f * jnp.log(jnp.sin(angles))[None, :]
    )
    block = math.gcd(degree_count, 16)
    state = pltpu.VMEM((order_count, lat_count), F32)
    return pl.pallas_call(
        legendre_kernel,
        grid=(degree_count // block,),
        in_specs=[
            pl.BlockSpec((order_count, lat_count), lambda i: (0, 0)),
            pl.BlockSpec((1, lat_count), lambda i: (0, 0)),
            pl.BlockSpec((order_count, 1), lambda i: (0, 0)),
            TOKEN_IN,
        ],
        out_specs=[
            pl.BlockSpec((order_count, block, lat_count), lambda i: (0, i, 0)),
            TOKEN_OUT,
        ],
        out_shape=[
            jax.ShapeDtypeStruct((order_count, degree_count, lat_count), BF16),
            TOKEN,
        ],
        scratch_shapes=[state, state, state, pltpu.VMEM((order_count, block, lat_count), F32)],
        compiler_params=PARAMS,
        cost_estimate=COST,
        name="legendre",
    )(start_log, jnp.cos(angles)[None, :], order_f, token)


def share_of(me_ref, piece, members, share):
    return pl.ds(pl.multiple_of(lax.rem(me_ref[0] + piece, members) * share, share), share)


def forward_row(me_ref, saved_ref, grid_ref, up_ref, down_ref, put):
    members = saved_ref.shape[1] // put.share
    for piece in range(members):
        place = share_of(me_ref, piece, members, put.share)
        v = dot(saved_ref[0, place, :], up_ref[...])
        tanh_part = jnp.tanh(kappa_gelu * (v + cubic_gelu * v * v * v))
        activation = (0.5 * v * (1.0 + tanh_part)).astype(BF16)
        total = grid_ref[0, place, :].astype(F32) + dot(activation, down_ref[...])
        put(piece, total.astype(BF16))


def cotangent_row(row, member_refs, target_ref, weight_ref, put):
    members = len(member_refs)
    weight_block = weight_ref[...]
    lane = lax.broadcasted_iota(jnp.int32, weight_block.shape, 1)
    weight = jnp.sum(jnp.where(lane == row, weight_block, 0.0), axis=1, keepdims=True)
    target = target_ref[0].astype(F32)
    values = [ref[...].reshape(target.shape).astype(F32) for ref in member_refs]
    pairs = {}
    for e in range(members):
        for f in range(e + 1, members):
            pairs[e, f] = slope_abs(values[e] - values[f])
    for e in range(members):
        total = None
        for f in range(members):
            if f == e:
                continue
            term = pairs[e, f] if e < f else -pairs[f, e]
            total = term if total is None else total + term
        direct = slope_abs(values[e] - target)
        put(
            e, (weight * (direct * (1.0 / members) - total * (1.0 / (members * members)))).astype(BF16)
        )


class Put:
    def __init__(self, refs, slot, back):
        self.refs, self.slot, self.back = refs, slot, back
        self.share = refs[0].shape[2]

    def __call__(self, piece, value):
        members = len(self.refs)
        self.refs[(members - piece) % members if self.back else piece][self.slot, 0] = value


def exchange_kernel(members, forward, cotangent, me_ref, *refs):
    refs = list(refs)
    take = lambda count: [refs.pop(0) for _ in range(count)]
    refs.pop(0)
    forward_refs = take(4) if forward is not None else None
    if cotangent is not None:
        target_ref, weight_ref = take(2)
        member_refs = take(members)
    out_refs = take(members)
    put_token(refs[0])
    if forward is not None:
        forward_row(me_ref, *forward_refs, Put(out_refs, 0, False))
    if cotangent is not None:
        put = Put(out_refs, 0 if forward is None else 1, True)
        row = cotangent + pl.program_id(0)
        cotangent_row(row, member_refs, target_ref, weight_ref, put)


def pick(slot, share, channels):
    return pl.BlockSpec((1, 1, share, channels), lambda i, q: (slot, i, 0, 0))


def exchange_rows(
    token, rows, members, me, forward, cotangent, saved, grid_input, up_weight, down_weight, target, weights, values
):
    _, lon, channels = saved.shape
    hidden = up_weight.shape[1]
    share = lon // members
    in_specs, operands = [TOKEN_IN], [me, token]
    if forward is not None:
        row_spec = pl.BlockSpec((1, lon, channels), lambda i, q: (forward + i, 0, 0))
        in_specs += [
            row_spec,
            row_spec,
            pl.BlockSpec((channels, hidden), lambda i, q: (0, 0)),
            pl.BlockSpec((hidden, channels), lambda i, q: (0, 0)),
        ]
        operands += [saved, grid_input, up_weight, down_weight]
    if cotangent is not None:
        in_specs += [
            pl.BlockSpec((1, share, channels), lambda i, q: (cotangent + i, q[0], 0)),
            pl.BlockSpec((share, weights.shape[1]), lambda i, q: (q[0], 0)),
        ]
        in_specs += [pick(slot, share, channels) for _, slot in values]
        operands += [target, weights] + [array for array, _ in values]
    slots = (forward is not None) + (cotangent is not None)
    out_shape = jax.ShapeDtypeStruct((slots, rows, share, channels), BF16)
    return pl.pallas_call(
        functools.partial(exchange_kernel, members, forward, cotangent),
        grid_spec=pltpu.PrefetchScalarGridSpec(
            num_scalar_prefetch=1,
            grid=(rows,),
            in_specs=in_specs,
            out_specs=[pl.BlockSpec((slots, 1, share, channels), lambda i, q: (0, i, 0, 0))] * members
            + [TOKEN_OUT],
        ),
        out_shape=[out_shape] * members + [TOKEN],
        compiler_params=PARAMS,
        cost_estimate=COST,
        name="exchange",
    )(*operands)


def backward_kernel(me_ref, saved_ref, up_ref, down_t_ref, up_t_ref, synth_ref, _, __, *refs):
    members = len(refs) - 4
    out_ref, token_ref, mixed_ref, waves_ref = refs[members:]
    put_token(token_ref)
    lon, channels = mixed_ref.shape
    share = lon // members
    for piece in range(members):
        place = share_of(me_ref, piece, members, share)
        v = dot(saved_ref[0, place, :], up_ref[...])
        square = v * v
        half = 0.5 + 0.5 * jnp.tanh(v * (kappa_gelu + (kappa_gelu * cubic_gelu) * square))
        inner = v * (2.0 * kappa_gelu + (6.0 * kappa_gelu * cubic_gelu) * square)
        slopes = half * (1.0 + (1.0 - half) * inner)
        act_grad = dot(refs[piece][0, 0], down_t_ref[...])
        pre_grad = (act_grad * slopes).astype(BF16)
        mixed_ref[place, :] = dot(pre_grad, up_t_ref[...]).astype(BF16)
    wave = dot(synth_ref[...], mixed_ref[...])
    modes = wave.shape[0] // 2
    row = pl.program_id(0)
    rows = out_ref.shape[2]
    place = pl.ds(row, modes, stride=rows)
    lanes = waves_ref.shape[2]
    for index in range(waves_ref.shape[0]):
        part, lane = divmod(index * lanes, channels)
        waves_ref[index, place, :] = wave[part * modes : (part + 1) * modes, lane : lane + lanes]

    @pl.when(row == rows - 1)
    def _():
        for index in range(waves_ref.shape[0]):
            block = waves_ref[index].reshape(out_ref.shape[:3] + (lanes,))
            out_ref[..., index * lanes : (index + 1) * lanes] = block.astype(BF16)


def backward_rows(token, ahead, first, groups, me, cot, saved, up_weight, down_t, up_t, synth):
    members = len(cot)
    _, rows, share, channels = cot[0][0].shape
    lon = saved.shape[1]
    modes = synth.shape[0] // 2
    whole = lambda a: pl.BlockSpec(a.shape, lambda i, q: (0, 0))
    out_shape = (groups, modes // groups, rows, 2 * channels)
    return pl.pallas_call(
        backward_kernel,
        grid_spec=pltpu.PrefetchScalarGridSpec(
            num_scalar_prefetch=1,
            grid=(rows,),
            in_specs=[
                pl.BlockSpec((1, lon, channels), lambda i, q: (first + i, 0, 0)),
                whole(up_weight),
                whole(down_t),
                whole(up_t),
                whole(synth),
                TOKEN_IN,
                TOKEN_IN,
            ]
            + [pick(slot, share, channels) for _, slot in cot],
            out_specs=[pl.BlockSpec(out_shape, lambda i, q: (0, 0, 0, 0)), TOKEN_OUT],
            scratch_shapes=[
                pltpu.VMEM((lon, channels), BF16),
                strips(modes * rows, 2 * channels),
            ],
        ),
        out_shape=[jax.ShapeDtypeStruct(out_shape, BF16), TOKEN],
        compiler_params=PARAMS,
        cost_estimate=COST,
        name="backward",
    )(me, saved, up_weight, down_t, up_t, synth, token, ahead, *[array for array, _ in cot])


def latitude(joined, table, quad, coeff, out_ref, m):
    groups, _, rows, columns = out_ref.shape
    lat = lax.dot_general(table, coeff, (((0,), (0,)), ((), ())), preferred_element_type=F32)
    lat = (lat * quad).reshape(joined, groups, rows // joined, columns)
    out_ref[:, m] = jnp.concatenate([lat[p] for p in range(joined)], axis=1).astype(BF16)


def spectral_kernel(parts, joined, table_ref, gain_ref, mix_t_ref, quad_ref, _, *refs):
    out_ref, lat_ref, token_ref = refs[parts:]
    put_token(token_ref)
    channels = mix_t_ref.shape[0]
    batch, columns = refs[0].shape[1], refs[0].shape[-1]
    first = quad_ref.shape[0]
    for m in range(batch):
        pieces = [refs[p][:, m].astype(F32).reshape(-1, columns) for p in range(parts)]
        wave = jnp.concatenate(pieces, axis=0).astype(BF16)
        gained = (dot(table_ref[m], wave) * gain_ref[...]).astype(BF16)
        coeff = jnp.concatenate(
            [
                dot(gained[:, :channels], mix_t_ref[...]).astype(BF16),
                dot(gained[:, channels:], mix_t_ref[...]).astype(BF16),
            ],
            axis=1,
        )
        out_ref[m] = coeff
        latitude(joined, table_ref[m, :, :first], quad_ref[...], coeff, lat_ref, m)


def spectral(token, joined, table, gain, mix_t, quad, waves):
    parts = len(waves)
    groups, modes, rows, columns = waves[0].shape
    degrees, lats = table.shape[1:]
    batch = math.gcd(modes, 4)
    lat_rows = joined * rows
    return pl.pallas_call(
        functools.partial(spectral_kernel, parts, joined),
        grid=(modes // batch,),
        in_specs=[
            pl.BlockSpec((batch, degrees, lats), lambda m: (m, 0, 0)),
            pl.BlockSpec(gain.shape, lambda m: (0, 0)),
            pl.BlockSpec(mix_t.shape, lambda m: (0, 0)),
            pl.BlockSpec(quad.shape, lambda m: (0, 0)),
            TOKEN_IN,
        ]
        + [pl.BlockSpec((groups, batch, rows, columns), lambda m: (0, m, 0, 0))] * parts,
        out_specs=[
            pl.BlockSpec((batch, degrees, columns), lambda m: (m, 0, 0)),
            pl.BlockSpec((groups, batch, lat_rows, columns), lambda m: (0, m, 0, 0)),
            TOKEN_OUT,
        ],
        out_shape=[
            jax.ShapeDtypeStruct((modes, degrees, columns), BF16),
            jax.ShapeDtypeStruct((groups, modes, lat_rows, columns), BF16),
            TOKEN,
        ],
        compiler_params=PARAMS,
        cost_estimate=COST,
        name="spectral",
    )(table, gain, mix_t, quad, token, *waves)


def latitude_kernel(joined, table_ref, quad_ref, coeff_ref, _, out_ref, token_ref):
    put_token(token_ref)
    for m in range(out_ref.shape[1]):
        latitude(joined, table_ref[m], quad_ref[...], coeff_ref[m], out_ref, m)


def latitude_rows(token, index, joined, groups, table, quad, coeff):
    modes, degrees, columns = coeff.shape
    lats = quad.shape[0]
    batch = math.gcd(modes, 4)
    out_shape = (groups, modes, lats // groups, columns)
    return pl.pallas_call(
        functools.partial(latitude_kernel, joined),
        grid=(modes // batch,),
        in_specs=[
            pl.BlockSpec((batch, degrees, lats), lambda m: (m, 0, index)),
            pl.BlockSpec(quad.shape, lambda m: (0, 0)),
            pl.BlockSpec((batch, degrees, columns), lambda m: (m, 0, 0)),
            TOKEN_IN,
        ],
        out_specs=[
            pl.BlockSpec((groups, batch, lats // groups, columns), lambda m: (0, m, 0, 0)),
            TOKEN_OUT,
        ],
        out_shape=[jax.ShapeDtypeStruct(out_shape, BF16), TOKEN],
        compiler_params=PARAMS,
        cost_estimate=COST,
        name="latitude",
    )(table, quad, coeff, token)


def output_kernel(joined, members, scale, me_ref, wave_ref, analysis_ref, _, *refs):
    out_ref, token_ref, waves_ref = refs[-3:]
    put_token(token_ref)
    every, share = wave_ref.shape[2], refs[0].shape[2]
    rows = every // joined
    count, _, lanes = waves_ref.shape
    channels = out_ref.shape[-1]
    row = pl.program_id(0)

    @pl.when(row == 0)
    def _():
        for index in range(count):
            block = wave_ref[..., index * lanes : (index + 1) * lanes].astype(F32)
            waves_ref[index] = block.reshape(waves_ref.shape[1:])

    at = pl.ds(row, waves_ref.shape[1] // every, stride=every)
    strip = [waves_ref[index, at, :].astype(BF16) for index in range(count)]
    half = count // 2
    wave = jnp.concatenate(
        [jnp.concatenate(strip[:half], axis=1), jnp.concatenate(strip[half:], axis=1)], axis=0
    )
    for piece in range(members):
        place = share_of(me_ref, piece, members, share)
        spatial = dot(analysis_ref[place, :], wave)
        cot = refs[piece][0, 0]
        for part in range(1, joined):
            cot = jnp.where(row >= part * rows, refs[part * members + piece][0, 0], cot)
        out_ref[0, 0, place, :] = (cot.astype(F32) + spatial * scale).astype(BF16)


def output_rows(token, index, shape, me, wave, cots, analysis, held):
    groups, modes, rows, columns = wave.shape
    joined, members = len(cots), len(cots[0])
    _, each, share, channels = cots[0][0][0].shape
    lon = shape[2]
    in_specs = [
        pl.BlockSpec(wave.shape, lambda i, q: (0, 0, 0, 0)),
        pl.BlockSpec(analysis.shape, lambda i, q: (0, 0)),
        TOKEN_IN,
    ]
    operands = [me, wave, analysis, token]
    for part, cot in enumerate(cots):
        for array, slot in cot:
            place = lambda i, q, at=part * each, slot=slot: (slot, jnp.clip(i - at, 0, each - 1), 0, 0)
            in_specs.append(pl.BlockSpec((1, 1, share, channels), place))
            operands.append(array)
    aliases = {}
    if held is not None:
        in_specs.append(pl.BlockSpec(memory_space=pl.ANY))
        aliases = {len(operands): 0}
        operands.append(held)
    return pl.pallas_call(
        functools.partial(output_kernel, joined, members, 1.0 / lon),
        grid_spec=pltpu.PrefetchScalarGridSpec(
            num_scalar_prefetch=1,
            grid=(rows,),
            in_specs=in_specs,
            out_specs=[
                pl.BlockSpec((1, 1, lon, channels), lambda i, q: (0, index * rows + i, 0, 0)),
                TOKEN_OUT,
            ],
            scratch_shapes=[strips(groups * modes * rows, columns)],
        ),
        out_shape=[jax.ShapeDtypeStruct(shape, BF16), TOKEN],
        input_output_aliases=aliases,
        compiler_params=PARAMS,
        cost_estimate=COST,
        name="output",
    )(*operands)


def shift(pieces):
    members = len(pieces)
    moved = [pieces[0]]
    for piece in range(1, members):
        pairs = [(e, (e + piece) % members) for e in range(members)]
        moved.append(lax.ppermute(pieces[piece], "member", pairs))
    return moved


def after_kernel(*_):
    pass


def after(value, other):
    return pl.pallas_call(
        after_kernel,
        in_specs=[TOKEN_IN, TOKEN_IN],
        out_specs=TOKEN_IN,
        out_shape=jax.ShapeDtypeStruct(value.shape, value.dtype),
        input_output_aliases={0: 0},
        name="after",
    )(value, other)


def kernel_order(parts, ahead):
    order = [("exchange", -ahead), ("exchange", 1 - ahead), ("table", 0)]
    for step in range(2 - ahead, parts + 2):
        order.append(("exchange", step) if step < parts else None)
        order.append(("backward", step - 2) if step >= 2 else None)
    return [entry for entry in order if entry is not None]


def shards(
    grid_input, saved_mixed, target, land_weight, mix_weight, degree_gain, up_weight, down_weight
):
    rows_lat, lon_count, channel_count = grid_input.shape[1:]
    total_lat = degree_gain.shape[0]
    mode_count = lon_count // 2
    members = lax.axis_size("member")
    groups = lax.axis_size("lat")
    local_modes = mode_count // groups
    parts = math.gcd(rows_lat, 6)
    rows = rows_lat // parts
    starts = [part * rows for part in range(parts)]

    grid_rows = grid_input[0]
    saved_rows = saved_mixed[0]
    down_t = down_weight.T
    up_t = up_weight.T
    synth, analysis = fourier_tables(lon_count, mode_count)
    lat_start = lax.axis_index("lat") * rows_lat
    local_angles = ((lat_start + jnp.arange(rows_lat)).astype(F32) + 0.5) * (math.pi / total_lat)
    weights = (jnp.sin(local_angles)[:, None] * land_weight.astype(F32)).T
    me = lax.axis_index("member").astype(jnp.int32).reshape(1)

    lats = jnp.arange(total_lat).reshape(groups, parts, rows).swapaxes(0, 1).reshape(-1)
    angles = (lats.astype(F32) + 0.5) * (math.pi / total_lat)
    quad_weight = (jnp.sin(angles) * (math.pi / total_lat))[:, None]
    local_orders = lax.axis_index("lat") * local_modes + jnp.arange(local_modes)

    joined = 2 if parts % 2 == 0 else 1
    token = jnp.zeros(TOKEN.shape, F32)
    values, cots, waves = {}, {}, {}
    table = None
    ahead = 2
    for kind, part in kernel_order(parts, ahead):
        if kind == "table":
            table, token = legendre_table(token, local_orders, angles, total_lat)
        elif kind == "exchange":
            forward = part + ahead if part + ahead < parts else None
            cotangent = part if part >= 0 else None
            *pieces, token = exchange_rows(
                token,
                rows,
                members,
                me,
                None if forward is None else starts[forward],
                None if cotangent is None else starts[cotangent],
                saved_rows,
                grid_rows,
                up_weight,
                down_weight,
                target,
                weights,
                values.get(cotangent),
            )
            moved = shift(pieces)
            values[forward] = [(array, 0) for array in moved]
            slot = 0 if forward is None else 1
            cots[cotangent] = [(moved[-piece % members], slot) for piece in range(members)]
        else:
            wave, token = backward_rows(
                token,
                waves.get(part - 2, token),
                starts[part],
                groups,
                me,
                cots[part],
                saved_rows,
                up_weight,
                down_t,
                up_t,
                synth,
            )
            if part == parts - 1 and part > 0:
                wave = after(wave, waves[part - 1])
            waves[part] = lax.all_to_all(wave, "lat", 0, 0, tiled=True)
    waves = [waves[part] for part in range(parts)]
    steps = parts // joined
    quads = [
        lax.slice_in_dim(quad_weight, step * total_lat // steps, (step + 1) * total_lat // steps)
        for step in range(steps)
    ]
    coeff, wave, token = spectral(
        token, joined, table, degree_gain[:, None], mix_weight.T, quads[0], waves
    )
    result = None
    lat_waves = {0: lax.all_to_all(wave, "lat", 0, 0, tiled=True)}
    for step in range(steps + 1):
        if 0 < step < steps:
            wave, token = latitude_rows(token, step, joined, groups, table, quads[step], coeff)
            lat_waves[step] = lax.all_to_all(wave, "lat", 0, 0, tiled=True)
        if step > 0:
            result, token = output_rows(
                token,
                step - 1,
                grid_input.shape,
                me,
                lat_waves[step - 1],
                [cots[part] for part in range((step - 1) * joined, step * joined)],
                analysis,
                result,
            )
    return result


def solution(mesh):
    in_specs = (
        P("member", "lat", None, None),
        P("member", "lat", None, None),
        P("lat", None, None),
        P("lat", None),
        P(),
        P(),
        P(),
        P(),
    )
    out_specs = P("member", "lat", None, None)
    return jax.shard_map(shards, mesh=mesh, in_specs=in_specs, out_specs=out_specs, check_vma=False)
```

```python
import functools
import math

import jax
import jax.numpy as jnp
from jax import lax
from jax.experimental import pallas as pl
from jax.experimental.pallas import tpu as pltpu
from jax.sharding import PartitionSpec as P

kappa_gelu = 0.7978845608
cubic_gelu = 0.044715
smooth_square = 0.25
F32 = jnp.float32
BF16 = jnp.bfloat16
PARAMS = pltpu.CompilerParams(vmem_limit_bytes=48 * 1024 * 1024)


TOKEN = jax.ShapeDtypeStruct((8, 128), F32)
TOKEN_IN = pl.BlockSpec(memory_space=pl.ANY)
TOKEN_OUT = pl.BlockSpec((8, 128), lambda *_: (0, 0))


def strips(rows, columns):
    lanes = math.gcd(columns // 2, 128)
    return pltpu.VMEM((columns // lanes, rows, lanes), F32)


def put_token(token_ref):
    token_ref[...] = jnp.zeros_like(token_ref)


COST = pl.CostEstimate(flops=5 * 10**10, bytes_accessed=1000, transcendentals=0)


def dot(a, b):
    return jnp.dot(a, b, preferred_element_type=F32)


def slope_abs(difference):
    return difference * lax.rsqrt(difference * difference + smooth_square)


def fourier_tables(lon_count, mode_count):
    row = jnp.arange(2 * mode_count)
    part = row // mode_count
    orders = row % mode_count
    positions = jnp.arange(lon_count)
    phase = orders[:, None] * positions[None, :] % lon_count
    angle_grid = phase.astype(F32) * (2.0 * math.pi / lon_count)
    values = jnp.where(part[:, None] == 0, jnp.cos(angle_grid), -jnp.sin(angle_grid))
    factor = jnp.where(orders == 0, 1.0, 2.0).astype(F32)
    synth = (values * factor[:, None]).astype(BF16)
    return synth, values.T.astype(BF16)


def legendre_kernel(
    start_ref, cosine_ref, order_ref, _, out_ref, token_ref, older_ref, newer_ref, log_ref, rows_ref
):
    put_token(token_ref)
    block = out_ref.shape[1]
    order = order_ref[...]
    cosine = cosine_ref[...]

    @pl.when(pl.program_id(0) == 0)
    def _():
        older_ref[...] = jnp.zeros_like(older_ref)
        newer_ref[...] = jnp.zeros_like(newer_ref)
        log_ref[...] = start_ref[...]

    for offset in range(block):
        degree = (pl.program_id(0) * block + offset).astype(F32)
        below = degree - 1.0
        alpha = jnp.sqrt(
            jnp.maximum(4.0 * degree * degree - 1.0, 1.0)
            / jnp.maximum(degree * degree - order * order, 1.0)
        )
        beta = jnp.sqrt(
            jnp.maximum(below * below - order * order, 0.0)
            / jnp.maximum(4.0 * below * below - 1.0, 1.0)
        )
        newer = newer_ref[...]
        log_scale = log_ref[...]
        recurred = alpha * (cosine * newer - beta * older_ref[...])
        fresh = jnp.where(degree < order, 0.0, jnp.where(degree == order, 1.0, recurred))
        rows_ref[:, offset, :] = fresh * jnp.exp(log_scale)
        norm = jnp.where(degree < order, 1.0, jnp.maximum(jnp.abs(fresh), jnp.abs(newer)))
        older_ref[...] = newer / norm
        newer_ref[...] = fresh / norm
        log_ref[...] = log_scale + jnp.log(norm)
    out_ref[...] = rows_ref[...].astype(BF16)


def legendre_table(token, orders, angles, degree_count):
    lat_count = angles.shape[0]
    order_count = orders.shape[0]
    order_f = orders.astype(F32)[:, None]
    factor_index = jnp.arange(1, lat_count + 1).astype(F32)
    ratios = jnp.log((2.0 * factor_index - 1.0) / (2.0 * factor_index))
    partial_log = jnp.sum(jnp.where(factor_index[None, :] <= order_f, ratios[None, :], 0.0), axis=1)
    start_log = (
        0.5 * jnp.log(order_f + 0.5)
        + 0.5 * partial_log[:, None]
        + order_f * jnp.log(jnp.sin(angles))[None, :]
    )
    block = math.gcd(degree_count, 16)
    state = pltpu.VMEM((order_count, lat_count), F32)
    return pl.pallas_call(
        legendre_kernel,
        grid=(degree_count // block,),
        in_specs=[
            pl.BlockSpec((order_count, lat_count), lambda i: (0, 0)),
            pl.BlockSpec((1, lat_count), lambda i: (0, 0)),
            pl.BlockSpec((order_count, 1), lambda i: (0, 0)),
            TOKEN_IN,
        ],
        out_specs=[
            pl.BlockSpec((order_count, block, lat_count), lambda i: (0, i, 0)),
            TOKEN_OUT,
        ],
        out_shape=[
            jax.ShapeDtypeStruct((order_count, degree_count, lat_count), BF16),
            TOKEN,
        ],
        scratch_shapes=[state, state, state, pltpu.VMEM((order_count, block, lat_count), F32)],
        compiler_params=PARAMS,
        cost_estimate=COST,
        name="legendre",
    )(start_log, jnp.cos(angles)[None, :], order_f, token)


def share_of(me_ref, piece, members, share):
    return pl.ds(pl.multiple_of(lax.rem(me_ref[0] + piece, members) * share, share), share)


def forward_row(me_ref, saved_ref, grid_ref, up_ref, down_ref, put):
    members = saved_ref.shape[1] // put.share
    for piece in range(members):
        place = share_of(me_ref, piece, members, put.share)
        v = dot(saved_ref[0, place, :], up_ref[...])
        tanh_part = jnp.tanh(kappa_gelu * (v + cubic_gelu * v * v * v))
        activation = (0.5 * v * (1.0 + tanh_part)).astype(BF16)
        total = grid_ref[0, place, :].astype(F32) + dot(activation, down_ref[...])
        put(piece, total.astype(BF16))


def cotangent_row(row, member_refs, target_ref, weight_ref, put):
    members = len(member_refs)
    weight_block = weight_ref[...]
    lane = lax.broadcasted_iota(jnp.int32, weight_block.shape, 1)
    weight = jnp.sum(jnp.where(lane == row, weight_block, 0.0), axis=1, keepdims=True)
    target = target_ref[0].astype(F32)
    values = [ref[...].reshape(target.shape).astype(F32) for ref in member_refs]
    pairs = {}
    for e in range(members):
        for f in range(e + 1, members):
            pairs[e, f] = slope_abs(values[e] - values[f])
    for e in range(members):
        total = None
        for f in range(members):
            if f == e:
                continue
            term = pairs[e, f] if e < f else -pairs[f, e]
            total = term if total is None else total + term
        direct = slope_abs(values[e] - target)
        put(
            e, (weight * (direct * (1.0 / members) - total * (1.0 / (members * members)))).astype(BF16)
        )


class Put:
    def __init__(self, refs, slot, back):
        self.refs, self.slot, self.back = refs, slot, back
        self.share = refs[0].shape[2]

    def __call__(self, piece, value):
        members = len(self.refs)
        self.refs[(members - piece) % members if self.back else piece][self.slot, 0] = value


def exchange_kernel(members, forward, cotangent, me_ref, *refs):
    refs = list(refs)
    take = lambda count: [refs.pop(0) for _ in range(count)]
    refs.pop(0)
    forward_refs = take(4) if forward is not None else None
    if cotangent is not None:
        target_ref, weight_ref = take(2)
        member_refs = take(members)
    out_refs = take(members)
    put_token(refs[0])
    if forward is not None:
        forward_row(me_ref, *forward_refs, Put(out_refs, 0, False))
    if cotangent is not None:
        put = Put(out_refs, 0 if forward is None else 1, True)
        row = cotangent + pl.program_id(0)
        cotangent_row(row, member_refs, target_ref, weight_ref, put)


def pick(slot, share, channels):
    return pl.BlockSpec((1, 1, share, channels), lambda i, q: (slot, i, 0, 0))


def exchange_rows(
    token, rows, members, me, forward, cotangent, saved, grid_input, up_weight, down_weight, target, weights, values
):
    _, lon, channels = saved.shape
    hidden = up_weight.shape[1]
    share = lon // members
    in_specs, operands = [TOKEN_IN], [me, token]
    if forward is not None:
        row_spec = pl.BlockSpec((1, lon, channels), lambda i, q: (forward + i, 0, 0))
        in_specs += [
            row_spec,
            row_spec,
            pl.BlockSpec((channels, hidden), lambda i, q: (0, 0)),
            pl.BlockSpec((hidden, channels), lambda i, q: (0, 0)),
        ]
        operands += [saved, grid_input, up_weight, down_weight]
    if cotangent is not None:
        in_specs += [
            pl.BlockSpec((1, share, channels), lambda i, q: (cotangent + i, q[0], 0)),
            pl.BlockSpec((share, weights.shape[1]), lambda i, q: (q[0], 0)),
        ]
        in_specs += [pick(slot, share, channels) for _, slot in values]
        operands += [target, weights] + [array for array, _ in values]
    slots = (forward is not None) + (cotangent is not None)
    out_shape = jax.ShapeDtypeStruct((slots, rows, share, channels), BF16)
    return pl.pallas_call(
        functools.partial(exchange_kernel, members, forward, cotangent),
        grid_spec=pltpu.PrefetchScalarGridSpec(
            num_scalar_prefetch=1,
            grid=(rows,),
            in_specs=in_specs,
            out_specs=[pl.BlockSpec((slots, 1, share, channels), lambda i, q: (0, i, 0, 0))] * members
            + [TOKEN_OUT],
        ),
        out_shape=[out_shape] * members + [TOKEN],
        compiler_params=PARAMS,
        cost_estimate=COST,
        name="exchange",
    )(*operands)


def backward_kernel(me_ref, saved_ref, up_ref, down_t_ref, up_t_ref, synth_ref, _, __, *refs):
    members = len(refs) - 5
    out_ref, token_ref, cot_ref, mixed_ref, waves_ref = refs[members:]
    put_token(token_ref)
    lon, channels = mixed_ref.shape
    share = lon // members
    for piece in range(members):
        cot_ref[share_of(me_ref, piece, members, share), :] = refs[piece][0, 0]
    for start in range(0, lon, lon // 2):
        place = pl.ds(start, lon // 2)
        v = dot(saved_ref[0, place, :], up_ref[...])
        square = v * v
        half = 0.5 + 0.5 * jnp.tanh(v * (kappa_gelu + (kappa_gelu * cubic_gelu) * square))
        inner = v * (2.0 * kappa_gelu + (6.0 * kappa_gelu * cubic_gelu) * square)
        slopes = half * (1.0 + (1.0 - half) * inner)
        act_grad = dot(cot_ref[place, :], down_t_ref[...])
        pre_grad = (act_grad * slopes).astype(BF16)
        mixed_ref[place, :] = dot(pre_grad, up_t_ref[...]).astype(BF16)
    wave = dot(synth_ref[...], mixed_ref[...])
    modes = wave.shape[0] // 2
    row = pl.program_id(0)
    rows = out_ref.shape[2]
    place = pl.ds(row, modes, stride=rows)
    lanes = waves_ref.shape[2]
    for index in range(waves_ref.shape[0]):
        part, lane = divmod(index * lanes, channels)
        waves_ref[index, place, :] = wave[part * modes : (part + 1) * modes, lane : lane + lanes]

    @pl.when(row == rows - 1)
    def _():
        for index in range(waves_ref.shape[0]):
            block = waves_ref[index].reshape(out_ref.shape[:3] + (lanes,))
            out_ref[..., index * lanes : (index + 1) * lanes] = block.astype(BF16)


def backward_rows(token, ahead, first, groups, me, cot, saved, up_weight, down_t, up_t, synth):
    members = len(cot)
    _, rows, share, channels = cot[0][0].shape
    lon = saved.shape[1]
    modes = synth.shape[0] // 2
    whole = lambda a: pl.BlockSpec(a.shape, lambda i, q: (0, 0))
    out_shape = (groups, modes // groups, rows, 2 * channels)
    return pl.pallas_call(
        backward_kernel,
        grid_spec=pltpu.PrefetchScalarGridSpec(
            num_scalar_prefetch=1,
            grid=(rows,),
            in_specs=[
                pl.BlockSpec((1, lon, channels), lambda i, q: (first + i, 0, 0)),
                whole(up_weight),
                whole(down_t),
                whole(up_t),
                whole(synth),
                TOKEN_IN,
                TOKEN_IN,
            ]
            + [pick(slot, share, channels) for _, slot in cot],
            out_specs=[pl.BlockSpec(out_shape, lambda i, q: (0, 0, 0, 0)), TOKEN_OUT],
            scratch_shapes=[
                pltpu.VMEM((lon, channels), BF16),
                pltpu.VMEM((lon, channels), BF16),
                strips(modes * rows, 2 * channels),
            ],
        ),
        out_shape=[jax.ShapeDtypeStruct(out_shape, BF16), TOKEN],
        compiler_params=PARAMS,
        cost_estimate=COST,
        name="backward",
    )(me, saved, up_weight, down_t, up_t, synth, token, ahead, *[array for array, _ in cot])


def latitude(joined, table, quad, coeff, out_ref, m):
    groups, _, rows, columns = out_ref.shape
    lat = lax.dot_general(table, coeff, (((0,), (0,)), ((), ())), preferred_element_type=F32)
    lat = (lat * quad).reshape(joined, groups, rows // joined, columns)
    out_ref[:, m] = jnp.concatenate([lat[p] for p in range(joined)], axis=1).astype(BF16)


def spectral_kernel(parts, joined, table_ref, gain_ref, mix_t_ref, quad_ref, _, *refs):
    out_ref, lat_ref, token_ref = refs[parts:]
    put_token(token_ref)
    channels = mix_t_ref.shape[0]
    batch, columns = refs[0].shape[1], refs[0].shape[-1]
    first = quad_ref.shape[0]
    degrees = table_ref.shape[1]
    gained = []
    for m in range(batch):
        pieces = [refs[p][:, m].astype(F32).reshape(-1, columns) for p in range(parts)]
        wave = jnp.concatenate(pieces, axis=0).astype(BF16)
        gained.append((dot(table_ref[m], wave) * gain_ref[...]).astype(BF16))
    gained = jnp.concatenate(gained, axis=0)
    coeff = jnp.concatenate(
        [
            dot(gained[:, :channels], mix_t_ref[...]).astype(BF16),
            dot(gained[:, channels:], mix_t_ref[...]).astype(BF16),
        ],
        axis=1,
    )
    for m in range(batch):
        own = coeff[m * degrees : (m + 1) * degrees]
        out_ref[m] = own
        latitude(joined, table_ref[m, :, :first], quad_ref[...], own, lat_ref, m)


def spectral(token, joined, table, gain, mix_t, quad, waves):
    parts = len(waves)
    groups, modes, rows, columns = waves[0].shape
    degrees, lats = table.shape[1:]
    batch = math.gcd(modes, 4)
    lat_rows = joined * rows
    return pl.pallas_call(
        functools.partial(spectral_kernel, parts, joined),
        grid=(modes // batch,),
        in_specs=[
            pl.BlockSpec((batch, degrees, lats), lambda m: (m, 0, 0)),
            pl.BlockSpec(gain.shape, lambda m: (0, 0)),
            pl.BlockSpec(mix_t.shape, lambda m: (0, 0)),
            pl.BlockSpec(quad.shape, lambda m: (0, 0)),
            TOKEN_IN,
        ]
        + [pl.BlockSpec((groups, batch, rows, columns), lambda m: (0, m, 0, 0))] * parts,
        out_specs=[
            pl.BlockSpec((batch, degrees, columns), lambda m: (m, 0, 0)),
            pl.BlockSpec((groups, batch, lat_rows, columns), lambda m: (0, m, 0, 0)),
            TOKEN_OUT,
        ],
        out_shape=[
            jax.ShapeDtypeStruct((modes, degrees, columns), BF16),
            jax.ShapeDtypeStruct((groups, modes, lat_rows, columns), BF16),
            TOKEN,
        ],
        compiler_params=PARAMS,
        cost_estimate=COST,
        name="spectral",
    )(table, gain, mix_t, quad, token, *waves)


def latitude_kernel(joined, table_ref, quad_ref, coeff_ref, _, out_ref, token_ref):
    put_token(token_ref)
    for m in range(out_ref.shape[1]):
        latitude(joined, table_ref[m], quad_ref[...], coeff_ref[m], out_ref, m)


def latitude_rows(token, index, joined, groups, table, quad, coeff):
    modes, degrees, columns = coeff.shape
    lats = quad.shape[0]
    batch = math.gcd(modes, 4)
    out_shape = (groups, modes, lats // groups, columns)
    return pl.pallas_call(
        functools.partial(latitude_kernel, joined),
        grid=(modes // batch,),
        in_specs=[
            pl.BlockSpec((batch, degrees, lats), lambda m: (m, 0, index)),
            pl.BlockSpec(quad.shape, lambda m: (0, 0)),
            pl.BlockSpec((batch, degrees, columns), lambda m: (m, 0, 0)),
            TOKEN_IN,
        ],
        out_specs=[
            pl.BlockSpec((groups, batch, lats // groups, columns), lambda m: (0, m, 0, 0)),
            TOKEN_OUT,
        ],
        out_shape=[jax.ShapeDtypeStruct(out_shape, BF16), TOKEN],
        compiler_params=PARAMS,
        cost_estimate=COST,
        name="latitude",
    )(table, quad, coeff, token)


def output_kernel(joined, members, scale, me_ref, wave_ref, analysis_ref, _, *refs):
    out_ref, token_ref, waves_ref, spatial_ref = refs[-4:]
    put_token(token_ref)
    every, share = wave_ref.shape[2], refs[0].shape[2]
    rows = every // joined
    count, _, lanes = waves_ref.shape
    channels = out_ref.shape[-1]
    row = pl.program_id(0)

    @pl.when(row == 0)
    def _():
        for index in range(count):
            block = wave_ref[..., index * lanes : (index + 1) * lanes].astype(F32)
            waves_ref[index] = block.reshape(waves_ref.shape[1:])

    at = pl.ds(row, waves_ref.shape[1] // every, stride=every)
    strip = [waves_ref[index, at, :].astype(BF16) for index in range(count)]
    half = count // 2
    wave = jnp.concatenate(
        [jnp.concatenate(strip[:half], axis=1), jnp.concatenate(strip[half:], axis=1)], axis=0
    )
    spatial_ref[...] = dot(analysis_ref[...], wave)
    for piece in range(members):
        place = share_of(me_ref, piece, members, share)
        cot = refs[piece][0, 0]
        for part in range(1, joined):
            cot = jnp.where(row >= part * rows, refs[part * members + piece][0, 0], cot)
        out_ref[0, 0, place, :] = (cot.astype(F32) + spatial_ref[place, :] * scale).astype(BF16)


def output_rows(token, index, shape, me, wave, cots, analysis, held):
    groups, modes, rows, columns = wave.shape
    joined, members = len(cots), len(cots[0])
    _, each, share, channels = cots[0][0][0].shape
    lon = shape[2]
    in_specs = [
        pl.BlockSpec(wave.shape, lambda i, q: (0, 0, 0, 0)),
        pl.BlockSpec(analysis.shape, lambda i, q: (0, 0)),
        TOKEN_IN,
    ]
    operands = [me, wave, analysis, token]
    for part, cot in enumerate(cots):
        for array, slot in cot:
            place = lambda i, q, at=part * each, slot=slot: (slot, jnp.clip(i - at, 0, each - 1), 0, 0)
            in_specs.append(pl.BlockSpec((1, 1, share, channels), place))
            operands.append(array)
    aliases = {}
    if held is not None:
        in_specs.append(pl.BlockSpec(memory_space=pl.ANY))
        aliases = {len(operands): 0}
        operands.append(held)
    return pl.pallas_call(
        functools.partial(output_kernel, joined, members, 1.0 / lon),
        grid_spec=pltpu.PrefetchScalarGridSpec(
            num_scalar_prefetch=1,
            grid=(rows,),
            in_specs=in_specs,
            out_specs=[
                pl.BlockSpec((1, 1, lon, channels), lambda i, q: (0, index * rows + i, 0, 0)),
                TOKEN_OUT,
            ],
            scratch_shapes=[strips(groups * modes * rows, columns), pltpu.VMEM((lon, channels), F32)],
        ),
        out_shape=[jax.ShapeDtypeStruct(shape, BF16), TOKEN],
        input_output_aliases=aliases,
        compiler_params=PARAMS,
        cost_estimate=COST,
        name="output",
    )(*operands)


def shift(pieces):
    members = len(pieces)
    moved = [pieces[0]]
    for piece in range(1, members):
        pairs = [(e, (e + piece) % members) for e in range(members)]
        moved.append(lax.ppermute(pieces[piece], "member", pairs))
    return moved


def after_kernel(*_):
    pass


def after(values, *others):
    return pl.pallas_call(
        after_kernel,
        in_specs=[TOKEN_IN] * (len(values) + len(others)),
        out_specs=[TOKEN_IN] * len(values),
        out_shape=[jax.ShapeDtypeStruct(value.shape, value.dtype) for value in values],
        input_output_aliases={index: index for index in range(len(values))},
        name="after",
    )(*values, *others)


def kernel_order(parts, ahead):
    order = [("exchange", -ahead), ("exchange", 1 - ahead), ("table", 0)]
    for step in range(2 - ahead, parts + 2):
        order.append(("exchange", step) if step < parts else None)
        order.append(("backward", step - 2) if step >= 2 else None)
        order.append(("gate", 0) if step == parts - 1 else None)
    return [entry for entry in order if entry is not None]


def shards(
    grid_input, saved_mixed, target, land_weight, mix_weight, degree_gain, up_weight, down_weight
):
    rows_lat, lon_count, channel_count = grid_input.shape[1:]
    total_lat = degree_gain.shape[0]
    mode_count = lon_count // 2
    members = lax.axis_size("member")
    groups = lax.axis_size("lat")
    local_modes = mode_count // groups
    parts = math.gcd(rows_lat, 6)
    rows = rows_lat // parts
    starts = [part * rows for part in range(parts)]

    grid_rows = grid_input[0]
    saved_rows = saved_mixed[0]
    down_t = down_weight.T
    up_t = up_weight.T
    synth, analysis = fourier_tables(lon_count, mode_count)
    lat_start = lax.axis_index("lat") * rows_lat
    local_angles = ((lat_start + jnp.arange(rows_lat)).astype(F32) + 0.5) * (math.pi / total_lat)
    weights = (jnp.sin(local_angles)[:, None] * land_weight.astype(F32)).T
    me = lax.axis_index("member").astype(jnp.int32).reshape(1)

    lats = jnp.arange(total_lat).reshape(groups, parts, rows).swapaxes(0, 1).reshape(-1)
    angles = (lats.astype(F32) + 0.5) * (math.pi / total_lat)
    quad_weight = (jnp.sin(angles) * (math.pi / total_lat))[:, None]
    local_orders = lax.axis_index("lat") * local_modes + jnp.arange(local_modes)

    joined = 2 if parts % 2 == 0 else 1
    token = jnp.zeros(TOKEN.shape, F32)
    values, cots, waves = {}, {}, {}
    table = None
    ahead = 2
    for kind, part in kernel_order(parts, ahead):
        if kind == "table":
            table, token = legendre_table(token, local_orders, angles, total_lat)
        elif kind == "exchange":
            forward = part + ahead if part + ahead < parts else None
            cotangent = part if part >= 0 else None
            *pieces, token = exchange_rows(
                token,
                rows,
                members,
                me,
                None if forward is None else starts[forward],
                None if cotangent is None else starts[cotangent],
                saved_rows,
                grid_rows,
                up_weight,
                down_weight,
                target,
                weights,
                values.get(cotangent),
            )
            held = pieces
            if part == parts - 1:
                continue
        if kind == "gate":
            earlier = [array for array, _ in cots[parts - 2][1:]]
            *moved, token = after(held[1:] + [token], *earlier)
            held = held[:1] + moved
        if kind in ("exchange", "gate"):
            moved = shift(held)
            values[forward] = [(array, 0) for array in moved]
            slot = 0 if forward is None else 1
            cots[cotangent] = [(moved[-piece % members], slot) for piece in range(members)]
        if kind == "backward":
            wave, token = backward_rows(
                token,
                waves.get(part - 2, token),
                starts[part],
                groups,
                me,
                cots[part],
                saved_rows,
                up_weight,
                down_t,
                up_t,
                synth,
            )
            if part == parts - 1 and part > 0:
                [wave] = after([wave], waves[part - 1])
            waves[part] = lax.all_to_all(wave, "lat", 0, 0, tiled=True)
    waves = [waves[part] for part in range(parts)]
    steps = parts // joined
    quads = [
        lax.slice_in_dim(quad_weight, step * total_lat // steps, (step + 1) * total_lat // steps)
        for step in range(steps)
    ]
    coeff, wave, token = spectral(
        token, joined, table, degree_gain[:, None], mix_weight.T, quads[0], waves
    )
    result = None
    lat_waves = {0: lax.all_to_all(wave, "lat", 0, 0, tiled=True)}
    for step in range(steps + 1):
        if 0 < step < steps:
            wave, token = latitude_rows(token, step, joined, groups, table, quads[step], coeff)
            lat_waves[step] = lax.all_to_all(wave, "lat", 0, 0, tiled=True)
        if step > 0:
            result, token = output_rows(
                token,
                step - 1,
                grid_input.shape,
                me,
                lat_waves[step - 1],
                [cots[part] for part in range((step - 1) * joined, step * joined)],
                analysis,
                result,
            )
    return result


def solution(mesh):
    in_specs = (
        P("member", "lat", None, None),
        P("member", "lat", None, None),
        P("lat", None, None),
        P("lat", None),
        P(),
        P(),
        P(),
        P(),
    )
    out_specs = P("member", "lat", None, None)
    return jax.shard_map(shards, mesh=mesh, in_specs=in_specs, out_specs=out_specs, check_vma=False)
```

```python
import functools
import math

import jax
import jax.numpy as jnp
from jax import lax
from jax.experimental import pallas as pl
from jax.experimental.pallas import tpu as pltpu
from jax.sharding import PartitionSpec as P

kappa_gelu = 0.7978845608
cubic_gelu = 0.044715
smooth_square = 0.25
F32 = jnp.float32
BF16 = jnp.bfloat16
PARAMS = pltpu.CompilerParams(vmem_limit_bytes=48 * 1024 * 1024)


TOKEN = jax.ShapeDtypeStruct((8, 128), F32)
TOKEN_IN = pl.BlockSpec(memory_space=pl.ANY)
TOKEN_OUT = pl.BlockSpec((8, 128), lambda *_: (0, 0))


def strips(rows, columns):
    lanes = math.gcd(columns // 2, 128)
    return pltpu.VMEM((columns // lanes, rows, lanes), F32)


def put_token(token_ref):
    token_ref[...] = jnp.zeros_like(token_ref)


COST = pl.CostEstimate(flops=5 * 10**10, bytes_accessed=1000, transcendentals=0)


def dot(a, b):
    return jnp.dot(a, b, preferred_element_type=F32)


def slope_abs(difference):
    return difference * lax.rsqrt(difference * difference + smooth_square)


def fourier_tables(lon_count, mode_count):
    row = jnp.arange(2 * mode_count)
    part = row // mode_count
    orders = row % mode_count
    positions = jnp.arange(lon_count)
    phase = orders[:, None] * positions[None, :] % lon_count
    angle_grid = phase.astype(F32) * (2.0 * math.pi / lon_count)
    values = jnp.where(part[:, None] == 0, jnp.cos(angle_grid), -jnp.sin(angle_grid))
    factor = jnp.where(orders == 0, 1.0, 2.0).astype(F32)
    synth = (values * factor[:, None]).astype(BF16)
    return synth, values.T.astype(BF16)


def legendre_kernel(
    start_ref, cosine_ref, order_ref, _, out_ref, token_ref, older_ref, newer_ref, log_ref, rows_ref
):
    put_token(token_ref)
    block = out_ref.shape[1]
    order = order_ref[...]
    cosine = cosine_ref[...]

    @pl.when(pl.program_id(0) == 0)
    def _():
        older_ref[...] = jnp.zeros_like(older_ref)
        newer_ref[...] = jnp.zeros_like(newer_ref)
        log_ref[...] = start_ref[...]

    for offset in range(block):
        degree = (pl.program_id(0) * block + offset).astype(F32)
        below = degree - 1.0
        alpha = jnp.sqrt(
            jnp.maximum(4.0 * degree * degree - 1.0, 1.0)
            / jnp.maximum(degree * degree - order * order, 1.0)
        )
        beta = jnp.sqrt(
            jnp.maximum(below * below - order * order, 0.0)
            / jnp.maximum(4.0 * below * below - 1.0, 1.0)
        )
        newer = newer_ref[...]
        log_scale = log_ref[...]
        recurred = alpha * (cosine * newer - beta * older_ref[...])
        fresh = jnp.where(degree < order, 0.0, jnp.where(degree == order, 1.0, recurred))
        rows_ref[:, offset, :] = fresh * jnp.exp(log_scale)
        norm = jnp.where(degree < order, 1.0, jnp.maximum(jnp.abs(fresh), jnp.abs(newer)))
        older_ref[...] = newer / norm
        newer_ref[...] = fresh / norm
        log_ref[...] = log_scale + jnp.log(norm)
    out_ref[...] = rows_ref[...].astype(BF16)


def legendre_table(token, orders, angles, degree_count):
    lat_count = angles.shape[0]
    order_count = orders.shape[0]
    order_f = orders.astype(F32)[:, None]
    factor_index = jnp.arange(1, lat_count + 1).astype(F32)
    ratios = jnp.log((2.0 * factor_index - 1.0) / (2.0 * factor_index))
    partial_log = jnp.sum(jnp.where(factor_index[None, :] <= order_f, ratios[None, :], 0.0), axis=1)
    start_log = (
        0.5 * jnp.log(order_f + 0.5)
        + 0.5 * partial_log[:, None]
        + order_f * jnp.log(jnp.sin(angles))[None, :]
    )
    block = math.gcd(degree_count, 16)
    state = pltpu.VMEM((order_count, lat_count), F32)
    return pl.pallas_call(
        legendre_kernel,
        grid=(degree_count // block,),
        in_specs=[
            pl.BlockSpec((order_count, lat_count), lambda i: (0, 0)),
            pl.BlockSpec((1, lat_count), lambda i: (0, 0)),
            pl.BlockSpec((order_count, 1), lambda i: (0, 0)),
            TOKEN_IN,
        ],
        out_specs=[
            pl.BlockSpec((order_count, block, lat_count), lambda i: (0, i, 0)),
            TOKEN_OUT,
        ],
        out_shape=[
            jax.ShapeDtypeStruct((order_count, degree_count, lat_count), BF16),
            TOKEN,
        ],
        scratch_shapes=[state, state, state, pltpu.VMEM((order_count, block, lat_count), F32)],
        compiler_params=PARAMS,
        cost_estimate=COST,
        name="legendre",
    )(start_log, jnp.cos(angles)[None, :], order_f, token)


def share_of(me_ref, piece, members, share):
    return pl.ds(pl.multiple_of(lax.rem(me_ref[0] + piece, members) * share, share), share)


def forward_row(me_ref, saved_ref, grid_ref, up_ref, down_ref, put):
    members = saved_ref.shape[1] // put.share
    for piece in range(members):
        place = share_of(me_ref, piece, members, put.share)
        v = dot(saved_ref[0, place, :], up_ref[...])
        tanh_part = jnp.tanh(kappa_gelu * (v + cubic_gelu * v * v * v))
        activation = (0.5 * v * (1.0 + tanh_part)).astype(BF16)
        total = grid_ref[0, place, :].astype(F32) + dot(activation, down_ref[...])
        put(piece, total.astype(BF16))


def cotangent_row(row, member_refs, target_ref, weight_ref, put):
    members = len(member_refs)
    weight_block = weight_ref[...]
    lane = lax.broadcasted_iota(jnp.int32, weight_block.shape, 1)
    weight = jnp.sum(jnp.where(lane == row, weight_block, 0.0), axis=1, keepdims=True)
    target = target_ref[0].astype(F32)
    values = [ref[...].reshape(target.shape).astype(F32) for ref in member_refs]
    pairs = {}
    for e in range(members):
        for f in range(e + 1, members):
            pairs[e, f] = slope_abs(values[e] - values[f])
    for e in range(members):
        total = None
        for f in range(members):
            if f == e:
                continue
            term = pairs[e, f] if e < f else -pairs[f, e]
            total = term if total is None else total + term
        direct = slope_abs(values[e] - target)
        put(
            e, (weight * (direct * (1.0 / members) - total * (1.0 / (members * members)))).astype(BF16)
        )


class Put:
    def __init__(self, refs, slot, back):
        self.refs, self.slot, self.back = refs, slot, back
        self.share = refs[0].shape[2]

    def __call__(self, piece, value):
        members = len(self.refs)
        self.refs[(members - piece) % members if self.back else piece][self.slot, 0] = value


def exchange_kernel(members, forward, cotangent, me_ref, *refs):
    refs = list(refs)
    take = lambda count: [refs.pop(0) for _ in range(count)]
    refs.pop(0)
    forward_refs = take(4) if forward is not None else None
    if cotangent is not None:
        target_ref, weight_ref = take(2)
        member_refs = take(members)
    out_refs = take(members)
    put_token(refs[0])
    if forward is not None:
        forward_row(me_ref, *forward_refs, Put(out_refs, 0, False))
    if cotangent is not None:
        put = Put(out_refs, 0 if forward is None else 1, True)
        row = cotangent + pl.program_id(0)
        cotangent_row(row, member_refs, target_ref, weight_ref, put)


def pick(slot, share, channels, batch=1):
    return pl.BlockSpec((1, batch, share, channels), lambda i, q: (slot, i, 0, 0))


def exchange_rows(
    token, rows, members, me, forward, cotangent, saved, grid_input, up_weight, down_weight, target, weights, values
):
    _, lon, channels = saved.shape
    hidden = up_weight.shape[1]
    share = lon // members
    in_specs, operands = [TOKEN_IN], [me, token]
    if forward is not None:
        row_spec = pl.BlockSpec((1, lon, channels), lambda i, q: (forward + i, 0, 0))
        in_specs += [
            row_spec,
            row_spec,
            pl.BlockSpec((channels, hidden), lambda i, q: (0, 0)),
            pl.BlockSpec((hidden, channels), lambda i, q: (0, 0)),
        ]
        operands += [saved, grid_input, up_weight, down_weight]
    if cotangent is not None:
        in_specs += [
            pl.BlockSpec((1, share, channels), lambda i, q: (cotangent + i, q[0], 0)),
            pl.BlockSpec((share, weights.shape[1]), lambda i, q: (q[0], 0)),
        ]
        in_specs += [pick(slot, share, channels) for _, slot in values]
        operands += [target, weights] + [array for array, _ in values]
    slots = (forward is not None) + (cotangent is not None)
    out_shape = jax.ShapeDtypeStruct((slots, rows, share, channels), BF16)
    return pl.pallas_call(
        functools.partial(exchange_kernel, members, forward, cotangent),
        grid_spec=pltpu.PrefetchScalarGridSpec(
            num_scalar_prefetch=1,
            grid=(rows,),
            in_specs=in_specs,
            out_specs=[pl.BlockSpec((slots, 1, share, channels), lambda i, q: (0, i, 0, 0))] * members
            + [TOKEN_OUT],
        ),
        out_shape=[out_shape] * members + [TOKEN],
        compiler_params=PARAMS,
        cost_estimate=COST,
        name="exchange",
    )(*operands)


def backward_kernel(me_ref, saved_ref, up_ref, down_t_ref, up_t_ref, synth_ref, _, __, *refs):
    members = len(refs) - 4
    out_ref, token_ref, cot_ref, waves_ref = refs[members:]
    put_token(token_ref)
    batch, lon, channels = saved_ref.shape
    share = lon // members
    for b in range(batch):
        for piece in range(members):
            cot_ref[b, share_of(me_ref, piece, members, share), :] = refs[piece][0, b]
    mixed = []
    for b in range(batch):
        halves = []
        for start in range(0, lon, lon // 2):
            place = pl.ds(start, lon // 2)
            v = dot(saved_ref[b, place, :], up_ref[...])
            square = v * v
            half = 0.5 + 0.5 * jnp.tanh(v * (kappa_gelu + (kappa_gelu * cubic_gelu) * square))
            inner = v * (2.0 * kappa_gelu + (6.0 * kappa_gelu * cubic_gelu) * square)
            slopes = half * (1.0 + (1.0 - half) * inner)
            act_grad = dot(cot_ref[b, place, :], down_t_ref[...])
            pre_grad = (act_grad * slopes).astype(BF16)
            halves.append(dot(pre_grad, up_t_ref[...]).astype(BF16))
        mixed.append(jnp.concatenate(halves, axis=0))
    wave = dot(synth_ref[...], jnp.concatenate(mixed, axis=1))
    modes = wave.shape[0] // 2
    step = pl.program_id(0)
    rows = out_ref.shape[2]
    count, _, lanes = waves_ref.shape
    for b in range(batch):
        place = pl.ds(step * batch + b, modes, stride=rows)
        for index in range(count):
            part, lane = divmod(index * lanes, channels)
            lane += b * channels
            waves_ref[index, place, :] = wave[part * modes : (part + 1) * modes, lane : lane + lanes]

    @pl.when(step == pl.num_programs(0) - 1)
    def _():
        for index in range(count):
            block = waves_ref[index].reshape(out_ref.shape[:3] + (lanes,))
            out_ref[..., index * lanes : (index + 1) * lanes] = block.astype(BF16)


def backward_rows(token, ahead, first, groups, me, cot, saved, up_weight, down_t, up_t, synth):
    members = len(cot)
    _, rows, share, channels = cot[0][0].shape
    lon = saved.shape[1]
    modes = synth.shape[0] // 2
    batch = math.gcd(rows, 2)
    whole = lambda a: pl.BlockSpec(a.shape, lambda i, q: (0, 0))
    out_shape = (groups, modes // groups, rows, 2 * channels)
    return pl.pallas_call(
        backward_kernel,
        grid_spec=pltpu.PrefetchScalarGridSpec(
            num_scalar_prefetch=1,
            grid=(rows // batch,),
            in_specs=[
                pl.BlockSpec((batch, lon, channels), lambda i, q: (first // batch + i, 0, 0)),
                whole(up_weight),
                whole(down_t),
                whole(up_t),
                whole(synth),
                TOKEN_IN,
                TOKEN_IN,
            ]
            + [pick(slot, share, channels, batch) for _, slot in cot],
            out_specs=[pl.BlockSpec(out_shape, lambda i, q: (0, 0, 0, 0)), TOKEN_OUT],
            scratch_shapes=[
                pltpu.VMEM((batch, lon, channels), BF16),
                strips(modes * rows, 2 * channels),
            ],
        ),
        out_shape=[jax.ShapeDtypeStruct(out_shape, BF16), TOKEN],
        compiler_params=PARAMS,
        cost_estimate=COST,
        name="backward",
    )(me, saved, up_weight, down_t, up_t, synth, token, ahead, *[array for array, _ in cot])


def latitude(joined, table, quad, coeff, out_ref, m):
    groups, _, rows, columns = out_ref.shape
    lat = lax.dot_general(table, coeff, (((0,), (0,)), ((), ())), preferred_element_type=F32)
    lat = (lat * quad).reshape(joined, groups, rows // joined, columns)
    out_ref[:, m] = jnp.concatenate([lat[p] for p in range(joined)], axis=1).astype(BF16)


def spectral_kernel(parts, joined, table_ref, gain_ref, mix_t_ref, quad_ref, _, *refs):
    out_ref, lat_ref, token_ref = refs[parts:]
    put_token(token_ref)
    channels = mix_t_ref.shape[0]
    batch, columns = refs[0].shape[1], refs[0].shape[-1]
    first = quad_ref.shape[0]
    degrees = table_ref.shape[1]
    gained = []
    for m in range(batch):
        pieces = [refs[p][:, m].astype(F32).reshape(-1, columns) for p in range(parts)]
        wave = jnp.concatenate(pieces, axis=0).astype(BF16)
        gained.append((dot(table_ref[m], wave) * gain_ref[...]).astype(BF16))
    gained = jnp.concatenate(gained, axis=0)
    coeff = jnp.concatenate(
        [
            dot(gained[:, :channels], mix_t_ref[...]).astype(BF16),
            dot(gained[:, channels:], mix_t_ref[...]).astype(BF16),
        ],
        axis=1,
    )
    for m in range(batch):
        own = coeff[m * degrees : (m + 1) * degrees]
        out_ref[m] = own
        latitude(joined, table_ref[m, :, :first], quad_ref[...], own, lat_ref, m)


def spectral(token, joined, table, gain, mix_t, quad, waves):
    parts = len(waves)
    groups, modes, rows, columns = waves[0].shape
    degrees, lats = table.shape[1:]
    batch = math.gcd(modes, 4)
    lat_rows = joined * rows
    return pl.pallas_call(
        functools.partial(spectral_kernel, parts, joined),
        grid=(modes // batch,),
        in_specs=[
            pl.BlockSpec((batch, degrees, lats), lambda m: (m, 0, 0)),
            pl.BlockSpec(gain.shape, lambda m: (0, 0)),
            pl.BlockSpec(mix_t.shape, lambda m: (0, 0)),
            pl.BlockSpec(quad.shape, lambda m: (0, 0)),
            TOKEN_IN,
        ]
        + [pl.BlockSpec((groups, batch, rows, columns), lambda m: (0, m, 0, 0))] * parts,
        out_specs=[
            pl.BlockSpec((batch, degrees, columns), lambda m: (m, 0, 0)),
            pl.BlockSpec((groups, batch, lat_rows, columns), lambda m: (0, m, 0, 0)),
            TOKEN_OUT,
        ],
        out_shape=[
            jax.ShapeDtypeStruct((modes, degrees, columns), BF16),
            jax.ShapeDtypeStruct((groups, modes, lat_rows, columns), BF16),
            TOKEN,
        ],
        compiler_params=PARAMS,
        cost_estimate=COST,
        name="spectral",
    )(table, gain, mix_t, quad, token, *waves)


def latitude_kernel(joined, table_ref, quad_ref, coeff_ref, _, out_ref, token_ref):
    put_token(token_ref)
    for m in range(out_ref.shape[1]):
        latitude(joined, table_ref[m], quad_ref[...], coeff_ref[m], out_ref, m)


def latitude_rows(token, index, joined, groups, table, quad, coeff):
    modes, degrees, columns = coeff.shape
    lats = quad.shape[0]
    batch = math.gcd(modes, 4)
    out_shape = (groups, modes, lats // groups, columns)
    return pl.pallas_call(
        functools.partial(latitude_kernel, joined),
        grid=(modes // batch,),
        in_specs=[
            pl.BlockSpec((batch, degrees, lats), lambda m: (m, 0, index)),
            pl.BlockSpec(quad.shape, lambda m: (0, 0)),
            pl.BlockSpec((batch, degrees, columns), lambda m: (m, 0, 0)),
            TOKEN_IN,
        ],
        out_specs=[
            pl.BlockSpec((groups, batch, lats // groups, columns), lambda m: (0, m, 0, 0)),
            TOKEN_OUT,
        ],
        out_shape=[jax.ShapeDtypeStruct(out_shape, BF16), TOKEN],
        compiler_params=PARAMS,
        cost_estimate=COST,
        name="latitude",
    )(table, quad, coeff, token)


def output_kernel(joined, members, scale, me_ref, wave_ref, analysis_ref, _, *refs):
    out_ref, token_ref, waves_ref, spatial_ref = refs[-4:]
    put_token(token_ref)
    every, share = wave_ref.shape[2], refs[0].shape[2]
    rows = every // joined
    count, _, lanes = waves_ref.shape
    channels = out_ref.shape[-1]
    batch = out_ref.shape[1]
    step = pl.program_id(0)

    @pl.when(step == 0)
    def _():
        for index in range(count):
            block = wave_ref[..., index * lanes : (index + 1) * lanes].astype(F32)
            waves_ref[index] = block.reshape(waves_ref.shape[1:])

    half = count // 2
    columns = [[], []]
    for b in range(batch):
        at = pl.ds(step * batch + b, waves_ref.shape[1] // every, stride=every)
        for index in range(count):
            columns[index // half].append(waves_ref[index, at, :].astype(BF16))
    wave = jnp.concatenate([jnp.concatenate(column, axis=1) for column in columns], axis=0)
    spatial_ref[...] = dot(analysis_ref[...], wave)
    for b in range(batch):
        for piece in range(members):
            place = share_of(me_ref, piece, members, share)
            cot = refs[piece][0, b]
            for part in range(1, joined):
                cot = jnp.where(step * batch >= part * rows, refs[part * members + piece][0, b], cot)
            spatial = spatial_ref[place, b * channels : (b + 1) * channels]
            out_ref[0, b, place, :] = (cot.astype(F32) + spatial * scale).astype(BF16)


def output_rows(token, index, shape, me, wave, cots, analysis, held):
    groups, modes, rows, columns = wave.shape
    joined, members = len(cots), len(cots[0])
    _, each, share, channels = cots[0][0][0].shape
    lon = shape[2]
    batch = math.gcd(each, 4)
    in_specs = [
        pl.BlockSpec(wave.shape, lambda i, q: (0, 0, 0, 0)),
        pl.BlockSpec(analysis.shape, lambda i, q: (0, 0)),
        TOKEN_IN,
    ]
    operands = [me, wave, analysis, token]
    for part, cot in enumerate(cots):
        for array, slot in cot:
            place = lambda i, q, at=part * each // batch, slot=slot: (
                slot,
                jnp.clip(i - at, 0, each // batch - 1),
                0,
                0,
            )
            in_specs.append(pl.BlockSpec((1, batch, share, channels), place))
            operands.append(array)
    aliases = {}
    if held is not None:
        in_specs.append(pl.BlockSpec(memory_space=pl.ANY))
        aliases = {len(operands): 0}
        operands.append(held)
    return pl.pallas_call(
        functools.partial(output_kernel, joined, members, 1.0 / lon),
        grid_spec=pltpu.PrefetchScalarGridSpec(
            num_scalar_prefetch=1,
            grid=(rows // batch,),
            in_specs=in_specs,
            out_specs=[
                pl.BlockSpec(
                    (1, batch, lon, channels), lambda i, q: (0, index * (rows // batch) + i, 0, 0)
                ),
                TOKEN_OUT,
            ],
            scratch_shapes=[strips(groups * modes * rows, columns), pltpu.VMEM((lon, batch * channels), F32)],
        ),
        out_shape=[jax.ShapeDtypeStruct(shape, BF16), TOKEN],
        input_output_aliases=aliases,
        compiler_params=PARAMS,
        cost_estimate=COST,
        name="output",
    )(*operands)


def shift(pieces):
    members = len(pieces)
    moved = [pieces[0]]
    for piece in range(1, members):
        pairs = [(e, (e + piece) % members) for e in range(members)]
        moved.append(lax.ppermute(pieces[piece], "member", pairs))
    return moved


def after_kernel(*_):
    pass


def after(values, *others):
    return pl.pallas_call(
        after_kernel,
        in_specs=[TOKEN_IN] * (len(values) + len(others)),
        out_specs=[TOKEN_IN] * len(values),
        out_shape=[jax.ShapeDtypeStruct(value.shape, value.dtype) for value in values],
        input_output_aliases={index: index for index in range(len(values))},
        name="after",
    )(*values, *others)


def kernel_order(parts, ahead):
    order = [("exchange", step) for step in range(-ahead, parts)]
    order.insert(2, ("table", 0))
    for part in range(parts):
        place = order.index(("exchange", min(part + 2, parts - 1))) + 1
        order.insert(place if part + 2 < parts else len(order), ("backward", part))
    return order


def shards(
    grid_input, saved_mixed, target, land_weight, mix_weight, degree_gain, up_weight, down_weight
):
    rows_lat, lon_count, channel_count = grid_input.shape[1:]
    total_lat = degree_gain.shape[0]
    mode_count = lon_count // 2
    members = lax.axis_size("member")
    groups = lax.axis_size("lat")
    local_modes = mode_count // groups
    parts = math.gcd(rows_lat, 6)
    rows = rows_lat // parts
    starts = [part * rows for part in range(parts)]

    grid_rows = grid_input[0]
    saved_rows = saved_mixed[0]
    down_t = down_weight.T
    up_t = up_weight.T
    synth, analysis = fourier_tables(lon_count, mode_count)
    lat_start = lax.axis_index("lat") * rows_lat
    local_angles = ((lat_start + jnp.arange(rows_lat)).astype(F32) + 0.5) * (math.pi / total_lat)
    weights = (jnp.sin(local_angles)[:, None] * land_weight.astype(F32)).T
    me = lax.axis_index("member").astype(jnp.int32).reshape(1)

    lats = jnp.arange(total_lat).reshape(groups, parts, rows).swapaxes(0, 1).reshape(-1)
    angles = (lats.astype(F32) + 0.5) * (math.pi / total_lat)
    quad_weight = (jnp.sin(angles) * (math.pi / total_lat))[:, None]
    local_orders = lax.axis_index("lat") * local_modes + jnp.arange(local_modes)

    joined = 2 if parts % 2 == 0 else 1
    token = jnp.zeros(TOKEN.shape, F32)
    values, cots, waves = {}, {}, {}
    table = None
    ahead = min(3, parts)
    for kind, part in kernel_order(parts, ahead):
        if kind == "table":
            table, token = legendre_table(token, local_orders, angles, total_lat)
        elif kind == "exchange":
            forward = part + ahead if part + ahead < parts else None
            cotangent = part if part >= 0 else None
            *pieces, token = exchange_rows(
                token,
                rows,
                members,
                me,
                None if forward is None else starts[forward],
                None if cotangent is None else starts[cotangent],
                saved_rows,
                grid_rows,
                up_weight,
                down_weight,
                target,
                weights,
                values.get(cotangent),
            )
            moved = shift(pieces)
            values[forward] = [(array, 0) for array in moved]
            slot = 0 if forward is None else 1
            cots[cotangent] = [(moved[-piece % members], slot) for piece in range(members)]
        else:
            wave, token = backward_rows(
                token,
                waves.get(part - 2, token),
                starts[part],
                groups,
                me,
                cots[part],
                saved_rows,
                up_weight,
                down_t,
                up_t,
                synth,
            )
            if part == parts - 1 and part > 0:
                [wave] = after([wave], waves[part - 1])
            waves[part] = lax.all_to_all(wave, "lat", 0, 0, tiled=True)
    waves = [waves[part] for part in range(parts)]
    steps = parts // joined
    quads = [
        lax.slice_in_dim(quad_weight, step * total_lat // steps, (step + 1) * total_lat // steps)
        for step in range(steps)
    ]
    coeff, wave, token = spectral(
        token, joined, table, degree_gain[:, None], mix_weight.T, quads[0], waves
    )
    result = None
    lat_waves = {0: lax.all_to_all(wave, "lat", 0, 0, tiled=True)}
    for step in range(steps + 1):
        if 0 < step < steps:
            wave, token = latitude_rows(token, step, joined, groups, table, quads[step], coeff)
            lat_waves[step] = lax.all_to_all(wave, "lat", 0, 0, tiled=True)
        if step > 0:
            result, token = output_rows(
                token,
                step - 1,
                grid_input.shape,
                me,
                lat_waves[step - 1],
                [cots[part] for part in range((step - 1) * joined, step * joined)],
                analysis,
                result,
            )
    return result


def solution(mesh):
    in_specs = (
        P("member", "lat", None, None),
        P("member", "lat", None, None),
        P("lat", None, None),
        P("lat", None),
        P(),
        P(),
        P(),
        P(),
    )
    out_specs = P("member", "lat", None, None)
    return jax.shard_map(shards, mesh=mesh, in_specs=in_specs, out_specs=out_specs, check_vma=False)
```

```python
import functools
import math

import jax
import jax.numpy as jnp
from jax import lax
from jax.experimental import pallas as pl
from jax.experimental.pallas import tpu as pltpu
from jax.sharding import PartitionSpec as P

kappa_gelu = 0.7978845608
cubic_gelu = 0.044715
smooth_square = 0.25
F32 = jnp.float32
BF16 = jnp.bfloat16
PARAMS = pltpu.CompilerParams(vmem_limit_bytes=48 * 1024 * 1024)


TOKEN = jax.ShapeDtypeStruct((8, 128), F32)
TOKEN_IN = pl.BlockSpec(memory_space=pl.ANY)
TOKEN_OUT = pl.BlockSpec((8, 128), lambda *_: (0, 0))


def strips(rows, columns):
    lanes = math.gcd(columns // 2, 128)
    return pltpu.VMEM((columns // lanes, rows, lanes), F32)


def put_token(token_ref):
    token_ref[...] = jnp.zeros_like(token_ref)


COST = pl.CostEstimate(flops=5 * 10**10, bytes_accessed=1000, transcendentals=0)


def dot(a, b):
    return jnp.dot(a, b, preferred_element_type=F32)


def slope_abs(difference):
    return difference * lax.rsqrt(difference * difference + smooth_square)


def fourier_tables(lon_count, mode_count):
    row = jnp.arange(2 * mode_count)
    part = row // mode_count
    orders = row % mode_count
    positions = jnp.arange(lon_count)
    phase = orders[:, None] * positions[None, :] % lon_count
    angle_grid = phase.astype(F32) * (2.0 * math.pi / lon_count)
    values = jnp.where(part[:, None] == 0, jnp.cos(angle_grid), -jnp.sin(angle_grid))
    factor = jnp.where(orders == 0, 1.0, 2.0).astype(F32)
    synth = (values * factor[:, None]).astype(BF16)
    return synth, values.T.astype(BF16)


def legendre_kernel(
    start_ref, cosine_ref, order_ref, _, out_ref, token_ref, older_ref, newer_ref, log_ref, rows_ref
):
    put_token(token_ref)
    block = out_ref.shape[1]
    order = order_ref[...]
    cosine = cosine_ref[...]

    @pl.when(pl.program_id(0) == 0)
    def _():
        older_ref[...] = jnp.zeros_like(older_ref)
        newer_ref[...] = jnp.zeros_like(newer_ref)
        log_ref[...] = start_ref[...]

    for offset in range(block):
        degree = (pl.program_id(0) * block + offset).astype(F32)
        below = degree - 1.0
        alpha = jnp.sqrt(
            jnp.maximum(4.0 * degree * degree - 1.0, 1.0)
            / jnp.maximum(degree * degree - order * order, 1.0)
        )
        beta = jnp.sqrt(
            jnp.maximum(below * below - order * order, 0.0)
            / jnp.maximum(4.0 * below * below - 1.0, 1.0)
        )
        newer = newer_ref[...]
        log_scale = log_ref[...]
        recurred = alpha * (cosine * newer - beta * older_ref[...])
        fresh = jnp.where(degree < order, 0.0, jnp.where(degree == order, 1.0, recurred))
        rows_ref[:, offset, :] = fresh * jnp.exp(log_scale)
        norm = jnp.where(degree < order, 1.0, jnp.maximum(jnp.abs(fresh), jnp.abs(newer)))
        older_ref[...] = newer / norm
        newer_ref[...] = fresh / norm
        log_ref[...] = log_scale + jnp.log(norm)
    out_ref[...] = rows_ref[...].astype(BF16)


def legendre_table(token, orders, angles, degree_count):
    lat_count = angles.shape[0]
    order_count = orders.shape[0]
    order_f = orders.astype(F32)[:, None]
    factor_index = jnp.arange(1, lat_count + 1).astype(F32)
    ratios = jnp.log((2.0 * factor_index - 1.0) / (2.0 * factor_index))
    partial_log = jnp.sum(jnp.where(factor_index[None, :] <= order_f, ratios[None, :], 0.0), axis=1)
    start_log = (
        0.5 * jnp.log(order_f + 0.5)
        + 0.5 * partial_log[:, None]
        + order_f * jnp.log(jnp.sin(angles))[None, :]
    )
    block = math.gcd(degree_count, 16)
    state = pltpu.VMEM((order_count, lat_count), F32)
    return pl.pallas_call(
        legendre_kernel,
        grid=(degree_count // block,),
        in_specs=[
            pl.BlockSpec((order_count, lat_count), lambda i: (0, 0)),
            pl.BlockSpec((1, lat_count), lambda i: (0, 0)),
            pl.BlockSpec((order_count, 1), lambda i: (0, 0)),
            TOKEN_IN,
        ],
        out_specs=[
            pl.BlockSpec((order_count, block, lat_count), lambda i: (0, i, 0)),
            TOKEN_OUT,
        ],
        out_shape=[
            jax.ShapeDtypeStruct((order_count, degree_count, lat_count), BF16),
            TOKEN,
        ],
        scratch_shapes=[state, state, state, pltpu.VMEM((order_count, block, lat_count), F32)],
        compiler_params=PARAMS,
        cost_estimate=COST,
        name="legendre",
    )(start_log, jnp.cos(angles)[None, :], order_f, token)


def share_of(me_ref, piece, members, share):
    return pl.ds(pl.multiple_of(lax.rem(me_ref[0] + piece, members) * share, share), share)


def forward_row(me_ref, saved_ref, grid_ref, up_ref, down_ref, put):
    members = saved_ref.shape[1] // put.share
    for piece in range(members):
        place = share_of(me_ref, piece, members, put.share)
        v = dot(saved_ref[0, place, :], up_ref[...])
        tanh_part = jnp.tanh(kappa_gelu * (v + cubic_gelu * v * v * v))
        activation = (0.5 * v * (1.0 + tanh_part)).astype(BF16)
        total = grid_ref[0, place, :].astype(F32) + dot(activation, down_ref[...])
        put(piece, total.astype(BF16))


def cotangent_row(row, member_refs, target_ref, weight_ref, put):
    members = len(member_refs)
    weight_block = weight_ref[...]
    lane = lax.broadcasted_iota(jnp.int32, weight_block.shape, 1)
    weight = jnp.sum(jnp.where(lane == row, weight_block, 0.0), axis=1, keepdims=True)
    target = target_ref[0].astype(F32)
    values = [ref[...].reshape(target.shape).astype(F32) for ref in member_refs]
    pairs = {}
    for e in range(members):
        for f in range(e + 1, members):
            pairs[e, f] = slope_abs(values[e] - values[f])
    for e in range(members):
        total = None
        for f in range(members):
            if f == e:
                continue
            term = pairs[e, f] if e < f else -pairs[f, e]
            total = term if total is None else total + term
        direct = slope_abs(values[e] - target)
        put(
            e, (weight * (direct * (1.0 / members) - total * (1.0 / (members * members)))).astype(BF16)
        )


class Put:
    def __init__(self, refs, slot, back):
        self.refs, self.slot, self.back = refs, slot, back
        self.share = refs[0].shape[2]

    def __call__(self, piece, value):
        members = len(self.refs)
        self.refs[(members - piece) % members if self.back else piece][self.slot, 0] = value


def exchange_kernel(members, forward, cotangent, me_ref, *refs):
    refs = list(refs)
    take = lambda count: [refs.pop(0) for _ in range(count)]
    take(2)
    forward_refs = take(4) if forward is not None else None
    if cotangent is not None:
        target_ref, weight_ref = take(2)
        member_refs = take(members)
    out_refs = take(members)
    put_token(refs[0])
    if forward is not None:
        forward_row(me_ref, *forward_refs, Put(out_refs, 0, False))
    if cotangent is not None:
        put = Put(out_refs, 0 if forward is None else 1, True)
        row = cotangent + pl.program_id(0)
        cotangent_row(row, member_refs, target_ref, weight_ref, put)


def pick(slot, share, channels, batch=1):
    return pl.BlockSpec((1, batch, share, channels), lambda i, q: (slot, i, 0, 0))


def exchange_rows(
    token, ahead, rows, members, me, forward, cotangent, saved, grid_input, up_weight, down_weight, target, weights, values
):
    _, lon, channels = saved.shape
    hidden = up_weight.shape[1]
    share = lon // members
    in_specs, operands = [TOKEN_IN, TOKEN_IN], [me, token, ahead]
    if forward is not None:
        row_spec = pl.BlockSpec((1, lon, channels), lambda i, q: (forward + i, 0, 0))
        in_specs += [
            row_spec,
            row_spec,
            pl.BlockSpec((channels, hidden), lambda i, q: (0, 0)),
            pl.BlockSpec((hidden, channels), lambda i, q: (0, 0)),
        ]
        operands += [saved, grid_input, up_weight, down_weight]
    if cotangent is not None:
        in_specs += [
            pl.BlockSpec((1, share, channels), lambda i, q: (cotangent + i, q[0], 0)),
            pl.BlockSpec((share, weights.shape[1]), lambda i, q: (q[0], 0)),
        ]
        in_specs += [pick(slot, share, channels) for _, slot in values]
        operands += [target, weights] + [array for array, _ in values]
    slots = (forward is not None) + (cotangent is not None)
    out_shape = jax.ShapeDtypeStruct((slots, rows, share, channels), BF16)
    return pl.pallas_call(
        functools.partial(exchange_kernel, members, forward, cotangent),
        grid_spec=pltpu.PrefetchScalarGridSpec(
            num_scalar_prefetch=1,
            grid=(rows,),
            in_specs=in_specs,
            out_specs=[pl.BlockSpec((slots, 1, share, channels), lambda i, q: (0, i, 0, 0))] * members
            + [TOKEN_OUT],
        ),
        out_shape=[out_shape] * members + [TOKEN],
        compiler_params=PARAMS,
        cost_estimate=COST,
        name="exchange",
    )(*operands)


def backward_kernel(me_ref, saved_ref, up_ref, down_t_ref, up_t_ref, synth_ref, _, __, *refs):
    members = len(refs) - 4
    out_ref, token_ref, cot_ref, waves_ref = refs[members:]
    put_token(token_ref)
    batch, lon, channels = saved_ref.shape
    share = lon // members
    for b in range(batch):
        for piece in range(members):
            cot_ref[b, share_of(me_ref, piece, members, share), :] = refs[piece][0, b]
    mixed = []
    for b in range(batch):
        halves = []
        for start in range(0, lon, lon // 2):
            place = pl.ds(start, lon // 2)
            v = dot(saved_ref[b, place, :], up_ref[...])
            square = v * v
            half = 0.5 + 0.5 * jnp.tanh(v * (kappa_gelu + (kappa_gelu * cubic_gelu) * square))
            inner = v * (2.0 * kappa_gelu + (6.0 * kappa_gelu * cubic_gelu) * square)
            slopes = half * (1.0 + (1.0 - half) * inner)
            act_grad = dot(cot_ref[b, place, :], down_t_ref[...])
            pre_grad = (act_grad * slopes).astype(BF16)
            halves.append(dot(pre_grad, up_t_ref[...]).astype(BF16))
        mixed.append(jnp.concatenate(halves, axis=0))
    wave = dot(synth_ref[...], jnp.concatenate(mixed, axis=1))
    modes = wave.shape[0] // 2
    step = pl.program_id(0)
    rows = out_ref.shape[2]
    count, _, lanes = waves_ref.shape
    for b in range(batch):
        place = pl.ds(step * batch + b, modes, stride=rows)
        for index in range(count):
            part, lane = divmod(index * lanes, channels)
            lane += b * channels
            waves_ref[index, place, :] = wave[part * modes : (part + 1) * modes, lane : lane + lanes]

    @pl.when(step == pl.num_programs(0) - 1)
    def _():
        for index in range(count):
            block = waves_ref[index].reshape(out_ref.shape[:3] + (lanes,))
            out_ref[..., index * lanes : (index + 1) * lanes] = block.astype(BF16)


def backward_rows(token, ahead, first, groups, me, cot, saved, up_weight, down_t, up_t, synth):
    members = len(cot)
    _, rows, share, channels = cot[0][0].shape
    lon = saved.shape[1]
    modes = synth.shape[0] // 2
    batch = math.gcd(rows, 2)
    whole = lambda a: pl.BlockSpec(a.shape, lambda i, q: (0, 0))
    out_shape = (groups, modes // groups, rows, 2 * channels)
    return pl.pallas_call(
        backward_kernel,
        grid_spec=pltpu.PrefetchScalarGridSpec(
            num_scalar_prefetch=1,
            grid=(rows // batch,),
            in_specs=[
                pl.BlockSpec((batch, lon, channels), lambda i, q: (first // batch + i, 0, 0)),
                whole(up_weight),
                whole(down_t),
                whole(up_t),
                whole(synth),
                TOKEN_IN,
                TOKEN_IN,
            ]
            + [pick(slot, share, channels, batch) for _, slot in cot],
            out_specs=[pl.BlockSpec(out_shape, lambda i, q: (0, 0, 0, 0)), TOKEN_OUT],
            scratch_shapes=[
                pltpu.VMEM((batch, lon, channels), BF16),
                strips(modes * rows, 2 * channels),
            ],
        ),
        out_shape=[jax.ShapeDtypeStruct(out_shape, BF16), TOKEN],
        compiler_params=PARAMS,
        cost_estimate=COST,
        name="backward",
    )(me, saved, up_weight, down_t, up_t, synth, token, ahead, *[array for array, _ in cot])


def latitude(joined, table, quad, coeff, out_ref, m):
    groups, _, rows, columns = out_ref.shape
    lat = lax.dot_general(table, coeff, (((0,), (0,)), ((), ())), preferred_element_type=F32)
    lat = (lat * quad).reshape(joined, groups, rows // joined, columns)
    out_ref[:, m] = jnp.concatenate([lat[p] for p in range(joined)], axis=1).astype(BF16)


def spectral_kernel(parts, joined, table_ref, gain_ref, mix_t_ref, quad_ref, _, *refs):
    out_ref, lat_ref, token_ref = refs[parts:]
    put_token(token_ref)
    channels = mix_t_ref.shape[0]
    batch, columns = refs[0].shape[1], refs[0].shape[-1]
    first = quad_ref.shape[0]
    degrees = table_ref.shape[1]
    gained = []
    for m in range(batch):
        pieces = [refs[p][:, m].astype(F32).reshape(-1, columns) for p in range(parts)]
        wave = jnp.concatenate(pieces, axis=0).astype(BF16)
        gained.append((dot(table_ref[m], wave) * gain_ref[...]).astype(BF16))
    gained = jnp.concatenate(gained, axis=0)
    coeff = jnp.concatenate(
        [
            dot(gained[:, :channels], mix_t_ref[...]).astype(BF16),
            dot(gained[:, channels:], mix_t_ref[...]).astype(BF16),
        ],
        axis=1,
    )
    for m in range(batch):
        own = coeff[m * degrees : (m + 1) * degrees]
        out_ref[m] = own
        latitude(joined, table_ref[m, :, :first], quad_ref[...], own, lat_ref, m)


def spectral(token, joined, table, gain, mix_t, quad, waves):
    parts = len(waves)
    groups, modes, rows, columns = waves[0].shape
    degrees, lats = table.shape[1:]
    batch = math.gcd(modes, 4)
    lat_rows = joined * rows
    return pl.pallas_call(
        functools.partial(spectral_kernel, parts, joined),
        grid=(modes // batch,),
        in_specs=[
            pl.BlockSpec((batch, degrees, lats), lambda m: (m, 0, 0)),
            pl.BlockSpec(gain.shape, lambda m: (0, 0)),
            pl.BlockSpec(mix_t.shape, lambda m: (0, 0)),
            pl.BlockSpec(quad.shape, lambda m: (0, 0)),
            TOKEN_IN,
        ]
        + [pl.BlockSpec((groups, batch, rows, columns), lambda m: (0, m, 0, 0))] * parts,
        out_specs=[
            pl.BlockSpec((batch, degrees, columns), lambda m: (m, 0, 0)),
            pl.BlockSpec((groups, batch, lat_rows, columns), lambda m: (0, m, 0, 0)),
            TOKEN_OUT,
        ],
        out_shape=[
            jax.ShapeDtypeStruct((modes, degrees, columns), BF16),
            jax.ShapeDtypeStruct((groups, modes, lat_rows, columns), BF16),
            TOKEN,
        ],
        compiler_params=PARAMS,
        cost_estimate=COST,
        name="spectral",
    )(table, gain, mix_t, quad, token, *waves)


def latitude_kernel(joined, table_ref, quad_ref, coeff_ref, _, out_ref, token_ref):
    put_token(token_ref)
    for m in range(out_ref.shape[1]):
        latitude(joined, table_ref[m], quad_ref[...], coeff_ref[m], out_ref, m)


def latitude_rows(token, index, joined, groups, table, quad, coeff):
    modes, degrees, columns = coeff.shape
    lats = quad.shape[0]
    batch = math.gcd(modes, 4)
    out_shape = (groups, modes, lats // groups, columns)
    return pl.pallas_call(
        functools.partial(latitude_kernel, joined),
        grid=(modes // batch,),
        in_specs=[
            pl.BlockSpec((batch, degrees, lats), lambda m: (m, 0, index)),
            pl.BlockSpec(quad.shape, lambda m: (0, 0)),
            pl.BlockSpec((batch, degrees, columns), lambda m: (m, 0, 0)),
            TOKEN_IN,
        ],
        out_specs=[
            pl.BlockSpec((groups, batch, lats // groups, columns), lambda m: (0, m, 0, 0)),
            TOKEN_OUT,
        ],
        out_shape=[jax.ShapeDtypeStruct(out_shape, BF16), TOKEN],
        compiler_params=PARAMS,
        cost_estimate=COST,
        name="latitude",
    )(table, quad, coeff, token)


def output_kernel(joined, members, scale, me_ref, wave_ref, analysis_ref, _, *refs):
    out_ref, token_ref, waves_ref, spatial_ref = refs[-4:]
    put_token(token_ref)
    every, share = wave_ref.shape[2], refs[0].shape[2]
    rows = every // joined
    count, _, lanes = waves_ref.shape
    channels = out_ref.shape[-1]
    batch = out_ref.shape[1]
    step = pl.program_id(0)

    @pl.when(step == 0)
    def _():
        for index in range(count):
            block = wave_ref[..., index * lanes : (index + 1) * lanes].astype(F32)
            waves_ref[index] = block.reshape(waves_ref.shape[1:])

    half = count // 2
    columns = [[], []]
    for b in range(batch):
        at = pl.ds(step * batch + b, waves_ref.shape[1] // every, stride=every)
        for index in range(count):
            columns[index // half].append(waves_ref[index, at, :].astype(BF16))
    wave = jnp.concatenate([jnp.concatenate(column, axis=1) for column in columns], axis=0)
    spatial_ref[...] = dot(analysis_ref[...], wave)
    for b in range(batch):
        for piece in range(members):
            place = share_of(me_ref, piece, members, share)
            cot = refs[piece][0, b]
            for part in range(1, joined):
                cot = jnp.where(step * batch >= part * rows, refs[part * members + piece][0, b], cot)
            spatial = spatial_ref[place, b * channels : (b + 1) * channels]
            out_ref[0, b, place, :] = (cot.astype(F32) + spatial * scale).astype(BF16)


def output_rows(token, index, shape, me, wave, cots, analysis, held):
    groups, modes, rows, columns = wave.shape
    joined, members = len(cots), len(cots[0])
    _, each, share, channels = cots[0][0][0].shape
    lon = shape[2]
    batch = math.gcd(each, 4)
    in_specs = [
        pl.BlockSpec(wave.shape, lambda i, q: (0, 0, 0, 0)),
        pl.BlockSpec(analysis.shape, lambda i, q: (0, 0)),
        TOKEN_IN,
    ]
    operands = [me, wave, analysis, token]
    for part, cot in enumerate(cots):
        for array, slot in cot:
            place = lambda i, q, at=part * each // batch, slot=slot: (
                slot,
                jnp.clip(i - at, 0, each // batch - 1),
                0,
                0,
            )
            in_specs.append(pl.BlockSpec((1, batch, share, channels), place))
            operands.append(array)
    aliases = {}
    if held is not None:
        in_specs.append(pl.BlockSpec(memory_space=pl.ANY))
        aliases = {len(operands): 0}
        operands.append(held)
    return pl.pallas_call(
        functools.partial(output_kernel, joined, members, 1.0 / lon),
        grid_spec=pltpu.PrefetchScalarGridSpec(
            num_scalar_prefetch=1,
            grid=(rows // batch,),
            in_specs=in_specs,
            out_specs=[
                pl.BlockSpec(
                    (1, batch, lon, channels), lambda i, q: (0, index * (rows // batch) + i, 0, 0)
                ),
                TOKEN_OUT,
            ],
            scratch_shapes=[strips(groups * modes * rows, columns), pltpu.VMEM((lon, batch * channels), F32)],
        ),
        out_shape=[jax.ShapeDtypeStruct(shape, BF16), TOKEN],
        input_output_aliases=aliases,
        compiler_params=PARAMS,
        cost_estimate=COST,
        name="output",
    )(*operands)


def shift(pieces):
    members = len(pieces)
    moved = [pieces[0]]
    for piece in range(1, members):
        pairs = [(e, (e + piece) % members) for e in range(members)]
        moved.append(lax.ppermute(pieces[piece], "member", pairs))
    return moved


def after_kernel(*_):
    pass


def after(values, *others):
    return pl.pallas_call(
        after_kernel,
        in_specs=[TOKEN_IN] * (len(values) + len(others)),
        out_specs=[TOKEN_IN] * len(values),
        out_shape=[jax.ShapeDtypeStruct(value.shape, value.dtype) for value in values],
        input_output_aliases={index: index for index in range(len(values))},
        name="after",
    )(*values, *others)


def kernel_order(parts, ahead):
    order = [("exchange", step) for step in range(-ahead, parts)]
    order.insert(2, ("table", 0))
    for part in range(parts):
        place = order.index(("exchange", min(part + 2, parts - 1))) + 1
        order.insert(place if part + 2 < parts else len(order), ("backward", part))
    if parts > 2:
        order.remove(("exchange", parts - 1))
        order.insert(order.index(("backward", parts - 3)) + 1, ("exchange", parts - 1))
    return order


def shards(
    grid_input, saved_mixed, target, land_weight, mix_weight, degree_gain, up_weight, down_weight
):
    rows_lat, lon_count, channel_count = grid_input.shape[1:]
    total_lat = degree_gain.shape[0]
    mode_count = lon_count // 2
    members = lax.axis_size("member")
    groups = lax.axis_size("lat")
    local_modes = mode_count // groups
    parts = math.gcd(rows_lat, 6)
    rows = rows_lat // parts
    starts = [part * rows for part in range(parts)]

    grid_rows = grid_input[0]
    saved_rows = saved_mixed[0]
    down_t = down_weight.T
    up_t = up_weight.T
    synth, analysis = fourier_tables(lon_count, mode_count)
    lat_start = lax.axis_index("lat") * rows_lat
    local_angles = ((lat_start + jnp.arange(rows_lat)).astype(F32) + 0.5) * (math.pi / total_lat)
    weights = (jnp.sin(local_angles)[:, None] * land_weight.astype(F32)).T
    me = lax.axis_index("member").astype(jnp.int32).reshape(1)

    lats = jnp.arange(total_lat).reshape(groups, parts, rows).swapaxes(0, 1).reshape(-1)
    angles = (lats.astype(F32) + 0.5) * (math.pi / total_lat)
    quad_weight = (jnp.sin(angles) * (math.pi / total_lat))[:, None]
    local_orders = lax.axis_index("lat") * local_modes + jnp.arange(local_modes)

    joined = 2 if parts % 2 == 0 else 1
    token = jnp.zeros(TOKEN.shape, F32)
    values, cots, waves = {}, {}, {}
    table = None
    ahead = min(3, parts)
    for kind, part in kernel_order(parts, ahead):
        if kind == "table":
            table, token = legendre_table(token, local_orders, angles, total_lat)
        elif kind == "exchange":
            forward = part + ahead if part + ahead < parts else None
            cotangent = part if part >= 0 else None
            *pieces, token = exchange_rows(
                token,
                waves.get(part - 3, token) if part == parts - 1 else token,
                rows,
                members,
                me,
                None if forward is None else starts[forward],
                None if cotangent is None else starts[cotangent],
                saved_rows,
                grid_rows,
                up_weight,
                down_weight,
                target,
                weights,
                values.get(cotangent),
            )
            moved = shift(pieces)
            values[forward] = [(array, 0) for array in moved]
            slot = 0 if forward is None else 1
            cots[cotangent] = [(moved[-piece % members], slot) for piece in range(members)]
        else:
            wave, token = backward_rows(
                token,
                waves.get(part - 2, token),
                starts[part],
                groups,
                me,
                cots[part],
                saved_rows,
                up_weight,
                down_t,
                up_t,
                synth,
            )
            if part == parts - 1 and part > 0:
                [wave] = after([wave], waves[part - 1])
            waves[part] = lax.all_to_all(wave, "lat", 0, 0, tiled=True)
    waves = [waves[part] for part in range(parts)]
    steps = parts // joined
    quads = [
        lax.slice_in_dim(quad_weight, step * total_lat // steps, (step + 1) * total_lat // steps)
        for step in range(steps)
    ]
    coeff, wave, token = spectral(
        token, joined, table, degree_gain[:, None], mix_weight.T, quads[0], waves
    )
    result = None
    lat_waves = {0: lax.all_to_all(wave, "lat", 0, 0, tiled=True)}
    for step in range(steps + 1):
        if 0 < step < steps:
            wave, token = latitude_rows(token, step, joined, groups, table, quads[step], coeff)
            lat_waves[step] = lax.all_to_all(wave, "lat", 0, 0, tiled=True)
        if step > 0:
            result, token = output_rows(
                token,
                step - 1,
                grid_input.shape,
                me,
                lat_waves[step - 1],
                [cots[part] for part in range((step - 1) * joined, step * joined)],
                analysis,
                result,
            )
    return result


def solution(mesh):
    in_specs = (
        P("member", "lat", None, None),
        P("member", "lat", None, None),
        P("lat", None, None),
        P("lat", None),
        P(),
        P(),
        P(),
        P(),
    )
    out_specs = P("member", "lat", None, None)
    return jax.shard_map(shards, mesh=mesh, in_specs=in_specs, out_specs=out_specs, check_vma=False)
```
